32 devices in a mesh: lat: 4 (over y, x), lon: 8 (over z, core).
Axes of the slice: x: 2, y: 2, z: 4, core: 2. Of those that a mesh axis runs over, the one named last changes fastest.
Arguments:
- grid_feat: bfloat16 [64, 256, 1024], P('lat', 'lon'), may hold values from -40 to 40
- mesh_feat: bfloat16 [32, 128, 1024], P('lat', 'lon'), may hold values from -40 to 40
- edges: int32 [12, 64, 256], P(None, 'lat', 'lon'), may hold values from 0 to 4095, as said below
- edge_mask: int32 [12, 64, 256], P(None, 'lat', 'lon'), may hold values from 0 to 1, as said below
- w_query: bfloat16 [1024, 1024], replicated, may hold values from -0.1875 to 0.1875
- w_key: bfloat16 [1024, 1024], replicated, may hold values from -0.1875 to 0.1875
- w_value: bfloat16 [1024, 1024], replicated, may hold values from -0.1875 to 0.1875
- w_out: bfloat16 [1024, 1024], replicated, may hold values from -0.1875 to 0.1875
- cotangent: bfloat16 [64, 256, 1024], P('lat', 'lon'), may hold values from -6 to 6
Outputs:
- layer_out: bfloat16 [64, 256, 1024], P('lat', 'lon')
- grid_grad: bfloat16 [64, 256, 1024], P('lat', 'lon')
- mesh_grad: bfloat16 [32, 128, 1024], P('lat', 'lon')
The draws below stay inside these ranges and needn't reach their ends.
Inputs may be any that keep to these rules, and one draw needn't show every extreme that they name: edges[e,i,j] = r * 128 + c names a mesh node with 0 <= r < 32, |r - i // 2| <= 4, and c within 4 of j // 2 around the circle of 128 columns; the 12 slots of a grid point name distinct nodes, masked slots included. `edge_mask`: each grid point has 3 to 12 live slots, and they come first.
All inputs are finite; a program needn't handle non-finite values.
Results may differ from the reference program's by a relative error of at most 0.01.
The reference program's roundings to bfloat16 on the way (of `queries`, `probs_half`, `attended`, `d_attended`, `d_scores` and `d_query`) count: a program that leaves them out, or rounds other values in their place, can miss the bound.
Values may be sent and summed in bfloat16 or wider, within the bound.
A program may use at most 128 MiB of HBM per device.

```python
import math
import jax
import jax.numpy as jnp
from jax import lax

MODEL_WIDTH = 1024
HEAD_COUNT = 16
EDGE_SLOTS = 12
HALO_REACH = 4
MESH_LAT = 32
MESH_LON = 128
GRID_LAT = 64
GRID_LON = 256


def scaled_features(key, shape_rows, shape_cols):
    base = jnp.clip(jax.random.normal(jax.random.fold_in(key, 11), (shape_rows, shape_cols, MODEL_WIDTH), jnp.float32), -5.0, 5.0)
    return base.astype(jnp.bfloat16)


def draw_grid_feat(key, part):
    return scaled_features(jax.random.fold_in(key, 101), GRID_LAT, GRID_LON)


def draw_mesh_feat(key, part):
    return scaled_features(jax.random.fold_in(key, 202), MESH_LAT, MESH_LON)


def draw_edges(key, part):
    span = 2 * HALO_REACH + 1
    offset_count = span * span
    offset_id = jnp.arange(offset_count, dtype=jnp.int32)
    d_lat = offset_id // span - HALO_REACH
    d_lon = offset_id % span - HALO_REACH
    home_lat = jnp.arange(GRID_LAT, dtype=jnp.int32) // 2
    home_lon = jnp.arange(GRID_LON, dtype=jnp.int32) // 2
    node_lat = home_lat[:, None, None] + d_lat[None, None, :]
    inside = (node_lat >= 0) & (node_lat < MESH_LAT)
    noise = jax.random.randint(jax.random.fold_in(key, 31), (GRID_LAT, GRID_LON, offset_count), 0, 1 << 20)
    ranking = jnp.where(inside, noise * 128 + offset_id[None, None, :], -1)
    picked = lax.top_k(ranking, EDGE_SLOTS)[1]
    chosen_lat = home_lat[:, None, None] + jnp.take(d_lat, picked)
    chosen_lon = jnp.mod(home_lon[None, :, None] + jnp.take(d_lon, picked), MESH_LON)
    node_index = chosen_lat * MESH_LON + chosen_lon
    return jnp.transpose(node_index, (2, 0, 1)).astype(jnp.int32)


def draw_edge_mask(key, part):
    live_count = jax.random.randint(jax.random.fold_in(key, 41), (1, GRID_LAT, GRID_LON), 3, EDGE_SLOTS + 1)
    slot_id = jnp.arange(EDGE_SLOTS, dtype=jnp.int32)[:, None, None]
    return jnp.where(slot_id < live_count, 1, 0).astype(jnp.int32)


def block_levels(rng, dims, split, smallest, high):
    def one(dim, blocks):
        steps = jax.random.uniform(jax.random.fold_in(jax.random.fold_in(rng, 6), dim), (blocks,), jnp.float32, smallest / len(split), high / len(split))
        return jnp.repeat(jnp.exp(steps), dims[dim] // blocks).reshape((-1,) + (1,) * (len(dims) - dim - 1))

    gain = one(*split[0])
    for cut in split[1:]:
        gain = gain * one(*cut)
    return gain


def normal_values(stream_key, dims, scale, bound, shards=(), held_as=jnp.bfloat16):
    values = scale * jax.random.normal(stream_key, dims, jnp.float32)
    if shards:
        values = values * block_levels(stream_key, dims, shards, -0.22, 0.18)
    return jnp.clip(values, -bound, bound).astype(held_as)


def setup_inputs(seed: int = 0) -> dict:
    seeds = jax.random.split(jax.random.key(seed), 10)
    grid_feat = draw_grid_feat(jax.random.fold_in(seeds[9], 71), 0)
    mesh_feat = draw_mesh_feat(jax.random.fold_in(seeds[9], 71), 0)
    edges = draw_edges(jax.random.fold_in(seeds[9], 71), 0)
    edge_mask = draw_edge_mask(jax.random.fold_in(seeds[9], 71), 0)
    w_query = normal_values(seeds[4], (MODEL_WIDTH, MODEL_WIDTH), MODEL_WIDTH ** -0.5, 0.1875)
    w_key = normal_values(seeds[5], (MODEL_WIDTH, MODEL_WIDTH), MODEL_WIDTH ** -0.5, 0.1875)
    w_value = normal_values(seeds[6], (MODEL_WIDTH, MODEL_WIDTH), MODEL_WIDTH ** -0.5, 0.1875)
    w_out = normal_values(seeds[7], (MODEL_WIDTH, MODEL_WIDTH), MODEL_WIDTH ** -0.5, 0.1875)
    cotangent = normal_values(seeds[8], (GRID_LAT, GRID_LON, MODEL_WIDTH), 1.0, 6.0, ((0, 4), (1, 8)))
    return dict(grid_feat=grid_feat, mesh_feat=mesh_feat, edges=edges, edge_mask=edge_mask, w_query=w_query, w_key=w_key, w_value=w_value, w_out=w_out, cotangent=cotangent)


NEG_FILL = -1e+30

def reference(grid_feat, mesh_feat, edges, edge_mask, w_query, w_key, w_value, w_out, cotangent):
    width = grid_feat.shape[2]
    head_size = width // HEAD_COUNT
    score_scale = 1.0 / math.sqrt(head_size)
    node_count = MESH_LAT * MESH_LON
    mesh_flat = mesh_feat.reshape(node_count, width)
    key_all = lax.optimization_barrier(jnp.dot(mesh_flat, w_key, preferred_element_type=jnp.float32).astype(jnp.bfloat16))
    value_all = lax.optimization_barrier(jnp.dot(mesh_flat, w_value, preferred_element_type=jnp.float32).astype(jnp.bfloat16))
    edge_rows = jnp.transpose(edges, (1, 2, 0))
    live_rows = jnp.transpose(edge_mask, (1, 2, 0))

    def one_row(carry, inputs):
        key_grad, value_grad = carry
        feats, targets, live, cot_rows = inputs
        count = feats.shape[0]
        queries = lax.optimization_barrier(jnp.dot(feats, w_query, preferred_element_type=jnp.float32).astype(jnp.bfloat16))
        query_heads = queries.reshape(count, HEAD_COUNT, head_size).astype(jnp.float32)
        key_sel = key_all[targets].reshape(count, EDGE_SLOTS, HEAD_COUNT, head_size).astype(jnp.float32)
        value_sel = value_all[targets].reshape(count, EDGE_SLOTS, HEAD_COUNT, head_size).astype(jnp.float32)
        scores = jnp.einsum('nhd,nehd->nhe', query_heads, key_sel) * score_scale
        scores = jnp.where(live[:, None, :] > 0, scores, NEG_FILL)
        row_max = lax.optimization_barrier(jnp.max(scores, axis=2, keepdims=True))
        exp_scores = jnp.exp(scores - row_max)
        prob_full = exp_scores / lax.optimization_barrier(jnp.sum(exp_scores, axis=2, keepdims=True))
        probs_half = lax.optimization_barrier(prob_full.astype(jnp.bfloat16)).astype(jnp.float32)
        attended = jnp.einsum('nhe,nehd->nhd', probs_half, value_sel).astype(jnp.bfloat16).reshape(count, width)
        layer_out = (feats.astype(jnp.float32) + jnp.dot(attended, w_out, preferred_element_type=jnp.float32)).astype(jnp.bfloat16)
        d_attended = lax.optimization_barrier(jnp.dot(cot_rows, w_out.T, preferred_element_type=jnp.float32).astype(jnp.bfloat16))
        d_heads = d_attended.reshape(count, HEAD_COUNT, head_size).astype(jnp.float32)
        d_probs = jnp.einsum('nhd,nehd->nhe', d_heads, value_sel)
        centred = lax.optimization_barrier(jnp.sum(prob_full * d_probs, axis=2, keepdims=True))
        d_scores = lax.optimization_barrier((prob_full * (d_probs - centred) * score_scale).astype(jnp.bfloat16)).astype(jnp.float32)
        d_query = jnp.einsum('nhe,nehd->nhd', d_scores, key_sel).astype(jnp.bfloat16).reshape(count, width)
        grid_grad = (cot_rows.astype(jnp.float32) + jnp.dot(d_query, w_query.T, preferred_element_type=jnp.float32)).astype(jnp.bfloat16)
        key_terms = jnp.einsum('nhe,nhd->nehd', d_scores, query_heads).reshape(count * EDGE_SLOTS, width)
        value_terms = jnp.einsum('nhe,nhd->nehd', probs_half, d_heads).reshape(count * EDGE_SLOTS, width)
        flat_targets = targets.reshape(count * EDGE_SLOTS).astype(jnp.int32)
        key_grad = key_grad.at[flat_targets].add(key_terms)
        value_grad = value_grad.at[flat_targets].add(value_terms)
        return ((key_grad, value_grad), (layer_out, grid_grad))
    start = (jnp.zeros((node_count, width), jnp.float32), jnp.zeros((node_count, width), jnp.float32))
    (key_grad, value_grad), (layer_out, grid_grad) = lax.scan(one_row, start, (grid_feat, edge_rows, live_rows, cotangent))
    key_half = key_grad.astype(jnp.bfloat16)
    value_half = value_grad.astype(jnp.bfloat16)
    mesh_grad = jnp.dot(key_half, w_key.T, preferred_element_type=jnp.float32)
    mesh_grad = mesh_grad + jnp.dot(value_half, w_value.T, preferred_element_type=jnp.float32)
    mesh_grad = mesh_grad.astype(jnp.bfloat16).reshape(MESH_LAT, MESH_LON, width)
    return (layer_out, grid_grad, mesh_grad)
```

```python
import functools
import math

import jax
import jax.numpy as jnp
from jax import lax
from jax.experimental import pallas as pl
from jax.experimental.pallas import tpu as pltpu
from jax.sharding import PartitionSpec as P

HEAD_COUNT = 16
EDGE_SLOTS = 12
HALO_REACH = 4
TILE_MESH_ROWS = 2
NEG_FILL = -1e30

NN = (((1,), (0,)), ((), ()))
NT = (((1,), (1,)), ((), ()))
TN = (((0,), (0,)), ((), ()))


def mm(a, b, dims=NN):
    return lax.dot_general(a, b, dims, preferred_element_type=jnp.float32)


def attend_tiles(
    shape, slot_ref, q_ref, d_ref, k_ref, v_ref, att_ref, dq_ref, dk_ref, dv_ref, bias_ref
):
    mesh_rows, padded_cols, tile_points, head_size = shape
    tiles = mesh_rows // TILE_MESH_ROWS
    step_keys = TILE_MESH_ROWS * padded_cols
    keys = (TILE_MESH_ROWS + 2 * HALO_REACH) * padded_cols
    pair = 2 * head_size
    pairs = q_ref.shape[1] // pair
    scale = 1.0 / math.sqrt(head_size)
    low = (lax.broadcasted_iota(jnp.int32, (1, pair), 1) < head_size).astype(jnp.float32)
    high = (1.0 - low).astype(jnp.bfloat16)
    low = low.astype(jnp.bfloat16)
    dk_ref[...] = jnp.zeros_like(dk_ref)
    dv_ref[...] = jnp.zeros_like(dv_ref)

    def tile_step(tile, carry):
        rows = pl.ds(pl.multiple_of(tile * tile_points, tile_points), tile_points)
        window = pl.ds(pl.multiple_of(tile * step_keys, step_keys), keys)
        key_id = lax.broadcasted_iota(jnp.int32, (keys, tile_points), 0) + tile * step_keys
        linked = key_id == slot_ref[0:1, rows]
        for slot in range(1, EDGE_SLOTS):
            linked = linked | (key_id == slot_ref[slot : slot + 1, rows])
        bias_ref[...] = jnp.where(linked, 0.0, NEG_FILL)

        def split(block):
            return jnp.concatenate([block * low, block * high], axis=0)

        def joined(both):
            return jnp.concatenate(
                [both[:head_size, :tile_points], both[head_size:, tile_points:]], axis=0
            ).T

        def pair_step(index):
            lanes = pl.ds(pl.multiple_of(index * pair, pair), pair)
            q2 = split(q_ref[rows, lanes])
            d2 = split(d_ref[rows, lanes])
            k2 = k_ref[window, lanes]
            v2 = v_ref[window, lanes]
            bias = bias_ref[...]
            scores = mm(k2, q2, NT) + jnp.concatenate([bias, bias], axis=1)
            exps = jnp.exp(scores - jnp.max(scores, axis=0, keepdims=True))
            prob = exps * (1.0 / jnp.sum(exps, axis=0, keepdims=True))
            half = prob.astype(jnp.bfloat16)
            d_prob = mm(v2, d2, NT)
            centred = jnp.sum(prob * d_prob, axis=0, keepdims=True)
            d_score = (prob * (d_prob - centred)).astype(jnp.bfloat16)
            att_ref[rows, lanes] = joined(mm(v2, half, TN)).astype(att_ref.dtype)
            dq_ref[rows, lanes] = (joined(mm(k2, d_score, TN)) * scale).astype(dq_ref.dtype)
            dk_ref[window, lanes] += mm(d_score, q2)
            dv_ref[window, lanes] += mm(half, d2)

        def two_pairs(index, inner):
            pair_step(index * 2)
            pair_step(index * 2 + 1)
            return inner

        lax.fori_loop(0, pairs // 2, two_pairs, 0)
        return carry

    lax.fori_loop(0, tiles, tile_step, 0)


def attend_kernel(
    shape, slot_ref, q_ref, d_ref, k_ref, v_ref, att_ref, dq_ref, dk_out, dv_out, dk_ref, dv_ref, bias_ref
):
    attend_tiles(
        shape, slot_ref, q_ref, d_ref, k_ref, v_ref, att_ref, dq_ref, dk_ref, dv_ref, bias_ref
    )
    dk_out[...] = dk_ref[...].astype(dk_out.dtype)
    dv_out[...] = dv_ref[...].astype(dv_out.dtype)


def attend(shape, slots, queries, d_attended, keys, values):
    mesh_rows, padded_cols, tile_points, head_size = shape
    points, width = queries.shape
    window = (TILE_MESH_ROWS + 2 * HALO_REACH) * padded_cols
    vmem = pl.BlockSpec(memory_space=pltpu.VMEM)
    return pl.pallas_call(
        functools.partial(attend_kernel, shape),
        out_shape=(
            jax.ShapeDtypeStruct((points, width), jnp.bfloat16),
            jax.ShapeDtypeStruct((points, width), jnp.bfloat16),
            jax.ShapeDtypeStruct(keys.shape, jnp.bfloat16),
            jax.ShapeDtypeStruct(keys.shape, jnp.bfloat16),
        ),
        in_specs=[vmem] * 5,
        out_specs=(vmem,) * 4,
        scratch_shapes=[
            pltpu.VMEM(keys.shape, jnp.float32),
            pltpu.VMEM(keys.shape, jnp.float32),
            pltpu.VMEM((window, tile_points), jnp.float32),
        ],
        compiler_params=pltpu.CompilerParams(vmem_limit_bytes=40 * 2**20),
        cost_estimate=pl.CostEstimate(
            flops=12 * points * window * width,
            bytes_accessed=8 * points * width + 8 * keys.shape[0] * width,
            transcendentals=points * window * HEAD_COUNT,
        ),
    )(slots, queries, d_attended, keys, values)


def shifted(block, axis, step, periodic):
    count = lax.axis_size(axis)
    moves = []
    for source in range(count):
        target = source + step
        if periodic:
            moves.append((source, target % count))
        elif 0 <= target < count:
            moves.append((source, target))
    return lax.ppermute(block, axis, moves)


def local(grid_feat, mesh_feat, edges, edge_mask, w_query, w_key, w_value, w_out, cotangent):
    grid_rows, grid_cols, width = grid_feat.shape
    mesh_rows, mesh_cols, _ = mesh_feat.shape
    points = grid_rows * grid_cols
    head_size = width // HEAD_COUNT
    scale = 1.0 / math.sqrt(head_size)
    reach = HALO_REACH
    padded_rows = mesh_rows + 2 * reach
    padded_cols = mesh_cols + 2 * reach
    lon_total = mesh_cols * lax.axis_size("lon")
    tile_points = TILE_MESH_ROWS * (grid_rows // mesh_rows) * grid_cols
    shape = (mesh_rows, padded_cols, tile_points, head_size)

    below = shifted(mesh_feat[-reach:], "lat", 1, False)
    above = shifted(mesh_feat[:reach], "lat", -1, False)
    tall = jnp.concatenate([below, mesh_feat, above], axis=0)
    left = shifted(tall[:, -reach:], "lon", 1, True)
    right = shifted(tall[:, :reach], "lon", -1, True)
    padded_feat = jnp.concatenate([left, tall, right], axis=1).reshape(-1, width)

    lat_start = lax.axis_index("lat") * mesh_rows
    lon_start = lax.axis_index("lon") * mesh_cols
    targets = edges.reshape(EDGE_SLOTS, points)
    live = edge_mask.reshape(EDGE_SLOTS, points)
    target_lat = targets // lon_total - lat_start + reach
    target_lon = jnp.mod(targets % lon_total - lon_start + reach, lon_total)
    slots = jnp.where(live > 0, target_lat * padded_cols + target_lon, -1)

    grid_flat = grid_feat.reshape(points, width)
    cot_rows = cotangent.reshape(points, width)
    queries = (mm(grid_flat, w_query).astype(jnp.bfloat16).astype(jnp.float32) * scale).astype(
        jnp.bfloat16
    )
    d_attended = mm(cot_rows, w_out, NT).astype(jnp.bfloat16)
    keys = mm(padded_feat, w_key).astype(jnp.bfloat16)
    values = mm(padded_feat, w_value).astype(jnp.bfloat16)

    attended, d_query, d_keys, d_values = attend(shape, slots, queries, d_attended, keys, values)

    partial = (mm(d_keys, w_key, NT) + mm(d_values, w_value, NT)).reshape(
        padded_rows, padded_cols, width
    )
    rims = partial.astype(jnp.bfloat16)
    from_right = shifted(rims[:, :reach], "lon", -1, True).astype(jnp.float32)
    from_left = shifted(rims[:, -reach:], "lon", 1, True).astype(jnp.float32)
    middle = partial[:, reach:-reach]
    middle = middle + jnp.pad(from_left, ((0, 0), (0, mesh_cols - reach), (0, 0)))
    middle = middle + jnp.pad(from_right, ((0, 0), (mesh_cols - reach, 0), (0, 0)))
    lat_rims = middle.astype(jnp.bfloat16)
    from_above = shifted(lat_rims[:reach], "lat", -1, False).astype(jnp.float32)
    from_below = shifted(lat_rims[-reach:], "lat", 1, False).astype(jnp.float32)
    owned = middle[reach:-reach]
    owned = owned + jnp.pad(from_below, ((0, mesh_rows - reach), (0, 0), (0, 0)))
    owned = owned + jnp.pad(from_above, ((mesh_rows - reach, 0), (0, 0), (0, 0)))

    layer_out = (grid_flat.astype(jnp.float32) + mm(attended, w_out)).astype(jnp.bfloat16)
    grid_grad = (cot_rows.astype(jnp.float32) + mm(d_query, w_query, NT)).astype(jnp.bfloat16)
    return (
        layer_out.reshape(grid_feat.shape),
        grid_grad.reshape(grid_feat.shape),
        owned.astype(jnp.bfloat16),
    )


def solution(mesh):
    placed = (
        P("lat", "lon", None),
        P("lat", "lon", None),
        P(None, "lat", "lon"),
        P(None, "lat", "lon"),
        P(),
        P(),
        P(),
        P(),
        P("lat", "lon", None),
    )
    return jax.shard_map(
        local,
        mesh=mesh,
        in_specs=placed,
        out_specs=(P("lat", "lon", None), P("lat", "lon", None), P("lat", "lon", None)),
        check_vma=False,
    )
```

```python
import functools
import math

import jax
import jax.numpy as jnp
from jax import lax
from jax.experimental import pallas as pl
from jax.experimental.pallas import tpu as pltpu
from jax.sharding import PartitionSpec as P

HEAD_COUNT = 16
EDGE_SLOTS = 12
HALO_REACH = 4
TILE_MESH_ROWS = 2
ROW_GROUP = 16
PAIRS_UNROLLED = 4
NEG_FILL = -1e30

NN = (((1,), (0,)), ((), ()))
NT = (((1,), (1,)), ((), ()))
TN = (((0,), (0,)), ((), ()))


def mm(a, b, dims=NN):
    return lax.dot_general(a, b, dims, preferred_element_type=jnp.float32)


class Plan:
    def __init__(self, mesh_rows, mesh_cols, grid_rows, grid_cols, width, lat_count, lon_count):
        reach = HALO_REACH
        self.mesh_rows, self.mesh_cols = mesh_rows, mesh_cols
        self.grid_rows, self.grid_cols, self.width = grid_rows, grid_cols, width
        self.lat_count, self.lon_count = lat_count, lon_count
        self.head = width // HEAD_COUNT
        self.scale = 1.0 / math.sqrt(self.head)
        self.points = grid_rows * grid_cols
        self.own = mesh_rows * mesh_cols
        padded_rows = mesh_rows + 2 * reach
        self.mid = padded_rows * mesh_cols
        self.strip = padded_rows * reach
        self.nodes = self.mid + 2 * self.strip
        self.lat_rim = reach * mesh_cols
        self.lon_rim = mesh_rows * reach
        self.corner = reach * reach
        self.tiles = mesh_rows // TILE_MESH_ROWS
        self.tile_grid_rows = grid_rows // self.tiles
        self.tile_points = self.tile_grid_rows * grid_cols
        window_rows = TILE_MESH_ROWS + 2 * reach
        self.mid_step = TILE_MESH_ROWS * mesh_cols
        self.mid_keys = window_rows * mesh_cols
        self.side_step = TILE_MESH_ROWS * reach
        slack = max((tile * self.side_step) % ROW_GROUP for tile in range(self.tiles))
        covered = window_rows * reach + slack
        self.side_keys = min(self.strip, -(-covered // ROW_GROUP) * ROW_GROUP)
        self.keys = self.mid_keys + 2 * self.side_keys

    def side_start(self, tile):
        return (tile * self.side_step) // ROW_GROUP * ROW_GROUP

    def exchanges(self):
        mid, strip = self.mid, self.strip
        corner, lon_rim, lat_rim = self.corner, self.lon_rim, self.lat_rim
        left, right = mid, mid + strip
        return (
            (-1, 0, 0, lat_rim),
            (1, 0, mid - lat_rim, lat_rim),
            (0, -1, left + corner, lon_rim),
            (0, 1, right + corner, lon_rim),
            (-1, -1, left, corner),
            (1, -1, left + strip - corner, corner),
            (-1, 1, right, corner),
            (1, 1, right + strip - corner, corner),
        )


def pack_matrix(plan):
    rows = 2 * plan.lon_rim
    row = lax.broadcasted_iota(jnp.int32, (rows, plan.own), 0)
    node = lax.broadcasted_iota(jnp.int32, (rows, plan.own), 1)
    is_right = (row >= plan.lon_rim).astype(jnp.int32)
    within = row - is_right * plan.lon_rim
    mesh_row = within // HALO_REACH
    col = within - mesh_row * HALO_REACH + is_right * (plan.mesh_cols - HALO_REACH)
    hit = node == mesh_row * plan.mesh_cols + col
    return hit.astype(jnp.float32).astype(jnp.bfloat16)


def fill_slots(plan, lat_start, lon_start, edges_ref, mask_ref, slot_ref):
    reach, cols = HALO_REACH, plan.mesh_cols
    lon_total = plan.mesh_cols * plan.lon_count
    for tile in range(plan.tiles):
        rows = range(tile * plan.tile_grid_rows, (tile + 1) * plan.tile_grid_rows)
        target = jnp.concatenate([edges_ref[:, row, :] for row in rows], axis=1)
        live = jnp.concatenate([mask_ref[:, row, :] for row in rows], axis=1)
        if lon_total & (lon_total - 1):
            node_row = lax.div(target, jnp.full_like(target, lon_total))
        else:
            node_row = lax.shift_right_logical(
                target, jnp.full_like(target, lon_total.bit_length() - 1)
            )
        node_col = target - node_row * lon_total - lon_start + reach
        node_col = jnp.where(node_col < 0, node_col + lon_total, node_col)
        node_col = jnp.where(node_col >= lon_total, node_col - lon_total, node_col)
        node_row = node_row - lat_start + reach
        side = plan.mid_keys + node_row * reach - plan.side_start(tile)
        middle = node_row * cols + node_col - reach - tile * plan.mid_step
        right = side + plan.side_keys + node_col - cols - reach
        slot = jnp.where(
            node_col < reach, side + node_col, jnp.where(node_col < cols + reach, middle, right)
        )
        slot_ref[tile] = jnp.where(live > 0, slot, -1)


def attend_tiles(
    plan, slot_ref, q_ref, d_ref, k_ref, v_ref, att_ref, dq_ref, dk_ref, dv_ref, bias_ref
):
    head, tile_points = plan.head, plan.tile_points
    pair = 2 * head
    pairs = plan.width // pair
    low = (lax.broadcasted_iota(jnp.int32, (1, pair), 1) < head).astype(jnp.float32)
    high = (1.0 - low).astype(jnp.bfloat16)
    low = low.astype(jnp.bfloat16)
    dk_ref[...] = jnp.zeros_like(dk_ref)
    dv_ref[...] = jnp.zeros_like(dv_ref)

    def tile_step(tile, carry):
        rows = pl.ds(pl.multiple_of(tile * tile_points, tile_points), tile_points)
        side = plan.side_start(tile)
        windows = (
            (pl.ds(pl.multiple_of(tile * plan.mid_step, ROW_GROUP), plan.mid_keys), 0),
            (pl.ds(pl.multiple_of(plan.mid + side, ROW_GROUP), plan.side_keys), plan.mid_keys),
            (
                pl.ds(pl.multiple_of(plan.mid + plan.strip + side, ROW_GROUP), plan.side_keys),
                plan.mid_keys + plan.side_keys,
            ),
        )
        key_id = lax.broadcasted_iota(jnp.int32, (plan.keys, tile_points), 0)
        slots = slot_ref[tile]
        linked = key_id == slots[0:1]
        for slot in range(1, EDGE_SLOTS):
            linked = linked | (key_id == slots[slot : slot + 1])
        bias_ref[...] = jnp.where(linked, 0.0, NEG_FILL)

        def split(block):
            return jnp.concatenate([block * low, block * high], axis=0)

        def joined(both):
            return jnp.concatenate([both[:head, :tile_points], both[head:, tile_points:]], axis=0).T

        def window_of(ref, lanes):
            return jnp.concatenate([ref[window, lanes] for window, _ in windows], axis=0)

        def add_window(ref, lanes, block):
            for window, first in windows:
                ref[window, lanes] += block[first : first + window.size]

        def pair_step(index):
            lanes = pl.ds(pl.multiple_of(index * pair, pair), pair)
            q2 = split(q_ref[rows, lanes])
            d2 = split(d_ref[rows, lanes])
            k2 = window_of(k_ref, lanes)
            v2 = window_of(v_ref, lanes)
            bias = bias_ref[...]
            scores = mm(k2, q2, NT) + jnp.concatenate([bias, bias], axis=1)
            exps = jnp.exp(scores - jnp.max(scores, axis=0, keepdims=True))
            prob = exps * (1.0 / jnp.sum(exps, axis=0, keepdims=True))
            half = prob.astype(jnp.bfloat16)
            d_prob = mm(v2, d2, NT)
            centred = jnp.sum(prob * d_prob, axis=0, keepdims=True)
            d_score = (prob * (d_prob - centred)).astype(jnp.bfloat16)
            att_ref[rows, lanes] = joined(mm(v2, half, TN)).astype(att_ref.dtype)
            dq_ref[rows, lanes] = (joined(mm(k2, d_score, TN)) * plan.scale).astype(dq_ref.dtype)
            add_window(dk_ref, lanes, mm(d_score, q2))
            add_window(dv_ref, lanes, mm(half, d2))

        def some_pairs(index, inner):
            for offset in range(PAIRS_UNROLLED):
                pair_step(index * PAIRS_UNROLLED + offset)
            return inner

        lax.fori_loop(0, pairs // PAIRS_UNROLLED, some_pairs, 0)
        return carry

    lax.fori_loop(0, plan.tiles, tile_step, 0)


def column_tiles(width, body):
    tile = min(width, 256)

    def step(index, carry):
        body(pl.ds(pl.multiple_of(index * tile, tile), tile))
        return carry

    lax.fori_loop(0, width // tile, step, 0)


def layer_kernel(
    plan,
    grid_in, mesh_in, edges_in, mask_in, wq_in, wk_in, wv_in, wo_in, cot_in,
    out_ref, grid_grad_ref, mesh_grad_ref,
    grid_ref, cot_ref, edges_ref, mask_ref, wq_ref, wk_ref, wv_ref, wo_ref,
    feat_ref, pack_ref, slot_ref, q_ref, d_ref, k_ref, v_ref, att_ref, dq_ref,
    dk_ref, dv_ref, bias_ref, own_ref, part_ref, back_ref,
    load_sem, send_sem, recv_sem, back_send_sem, back_recv_sem,
):
    reach = HALO_REACH
    lat, lon = lax.axis_index("lat"), lax.axis_index("lon")
    exchanges = plan.exchanges()
    first_own = plan.lat_rim

    def device(lat_step, lon_step):
        return (
            lax.rem(lat + lat_step + plan.lat_count, plan.lat_count),
            lax.rem(lon + lon_step + plan.lon_count, plan.lon_count),
        )

    barrier = pltpu.get_barrier_semaphore()
    for lat_step, lon_step, _, _ in exchanges:
        pl.semaphore_signal(
            barrier, inc=1, device_id=device(lat_step, lon_step), device_id_type=pl.DeviceIdType.MESH
        )
    own_feat = feat_ref.at[pl.ds(first_own, plan.own)]
    loads = []
    for index, (source, target) in enumerate(
        (
            (mesh_in, own_feat), (grid_in, grid_ref), (wq_in, wq_ref), (edges_in, edges_ref),
            (mask_in, mask_ref), (cot_in, cot_ref), (wo_in, wo_ref), (wk_in, wk_ref),
            (wv_in, wv_ref),
        )
    ):
        load = pltpu.make_async_copy(source, target, load_sem.at[index])
        load.start()
        loads.append(load)
    mesh_load, grid_load, wq_load, edges_load, mask_load, cot_load, wo_load, wk_load, wv_load = loads

    mesh_load.wait()
    pack = pack_matrix(plan)
    pack_ref[...] = mm(pack, own_feat[...]).astype(jnp.bfloat16)
    pl.semaphore_wait(barrier, len(exchanges))
    corner, lon_rim = plan.corner, plan.lon_rim
    sent = []
    for index, (lat_step, lon_step, first, count) in enumerate(exchanges):
        if lon_step == 0:
            start = first_own + (plan.own - count if lat_step < 0 else 0)
            source = feat_ref.at[pl.ds(start, count)]
        else:
            start = lon_rim if lon_step < 0 else 0
            if lat_step < 0:
                start += lon_rim - count
            source = pack_ref.at[pl.ds(start, count)]
        copy = pltpu.make_async_remote_copy(
            src_ref=source,
            dst_ref=feat_ref.at[pl.ds(first, count)],
            send_sem=send_sem.at[index],
            recv_sem=recv_sem.at[index],
            device_id=device(-lat_step, -lon_step),
            device_id_type=pl.DeviceIdType.MESH,
        )
        copy.start()
        sent.append(copy)

    grid_load.wait()
    wq_load.wait()

    def query_columns(columns):
        queries = mm(grid_ref[...], wq_ref[:, columns]).astype(jnp.bfloat16)
        q_ref[:, columns] = (queries.astype(jnp.float32) * plan.scale).astype(jnp.bfloat16)

    column_tiles(plan.width, query_columns)
    edges_load.wait()
    mask_load.wait()
    fill_slots(
        plan, lat * plan.mesh_rows, lon * plan.mesh_cols, edges_ref, mask_ref, slot_ref
    )
    cot_load.wait()
    wo_load.wait()

    def d_columns(columns):
        d_ref[:, columns] = mm(cot_ref[...], wo_ref[columns, :], NT).astype(jnp.bfloat16)

    column_tiles(plan.width, d_columns)
    wk_load.wait()
    wv_load.wait()
    for copy in sent:
        copy.wait()

    def pair_columns(columns):
        feat = feat_ref[...]
        k_ref[:, columns] = mm(feat, wk_ref[:, columns]).astype(jnp.bfloat16)
        v_ref[:, columns] = mm(feat, wv_ref[:, columns]).astype(jnp.bfloat16)

    column_tiles(plan.width, pair_columns)
    attend_tiles(
        plan, slot_ref, q_ref, d_ref, k_ref, v_ref, att_ref, dq_ref, dk_ref, dv_ref, bias_ref
    )
    k_ref[...] = dk_ref[...].astype(jnp.bfloat16)
    v_ref[...] = dv_ref[...].astype(jnp.bfloat16)

    def part_columns(columns):
        part = mm(k_ref[...], wk_ref[columns, :], NT) + mm(v_ref[...], wv_ref[columns, :], NT)
        part_ref[:, columns] = part.astype(jnp.bfloat16)
        own_ref[:, columns] = part[first_own : first_own + plan.own]

    column_tiles(plan.width, part_columns)
    returned = []
    for index, (lat_step, lon_step, first, count) in enumerate(exchanges):
        if lon_step == 0:
            start = count if lat_step < 0 else 0
        else:
            base = 2 * plan.lat_rim
            if lat_step == 0:
                start = base + (lon_rim if lon_step < 0 else 0)
            else:
                base += 2 * lon_rim
                order = (0 if lon_step > 0 else 2) + (1 if lat_step < 0 else 0)
                start = base + order * corner
        copy = pltpu.make_async_remote_copy(
            src_ref=part_ref.at[pl.ds(first, count)],
            dst_ref=back_ref.at[pl.ds(start, count)],
            send_sem=back_send_sem.at[index],
            recv_sem=back_recv_sem.at[index],
            device_id=device(lat_step, lon_step),
            device_id_type=pl.DeviceIdType.MESH,
        )
        copy.start()
        returned.append(copy)

    def out_columns(columns):
        out = grid_ref[:, columns].astype(jnp.float32) + mm(att_ref[...], wo_ref[:, columns])
        out_ref[:, columns] = out.astype(jnp.bfloat16)
        grad = cot_ref[:, columns].astype(jnp.float32) + mm(dq_ref[...], wq_ref[columns, :], NT)
        grid_grad_ref[:, columns] = grad.astype(jnp.bfloat16)

    column_tiles(plan.width, out_columns)
    for copy in returned:
        copy.wait()
    corners = [
        pack[0:corner], pack[lon_rim - corner : lon_rim],
        pack[lon_rim : lon_rim + corner], pack[2 * lon_rim - corner : 2 * lon_rim],
    ]
    unpack = jnp.concatenate([pack] + corners, axis=0)
    lat_terms = 2 * plan.lat_rim
    last_rim = pl.ds(plan.own - plan.lat_rim, plan.lat_rim)

    def mesh_columns(columns):
        total = own_ref[:, columns] + mm(unpack, back_ref[lat_terms:, columns], TN)
        own_ref[:, columns] = total
        for start, rows in ((0, pl.ds(0, plan.lat_rim)), (plan.lat_rim, last_rim)):
            own_ref[rows, columns] += back_ref[pl.ds(start, plan.lat_rim), columns].astype(
                jnp.float32
            )
        mesh_grad_ref[:, columns] = own_ref[:, columns].astype(jnp.bfloat16)

    column_tiles(plan.width, mesh_columns)


def local(grid_feat, mesh_feat, edges, edge_mask, w_query, w_key, w_value, w_out, cotangent):
    grid_rows, grid_cols, width = grid_feat.shape
    mesh_rows, mesh_cols, _ = mesh_feat.shape
    plan = Plan(
        mesh_rows, mesh_cols, grid_rows, grid_cols, width, lax.axis_size("lat"), lax.axis_size("lon")
    )
    half, full = jnp.bfloat16, jnp.float32
    points, own, nodes = plan.points, plan.own, plan.nodes
    anywhere = pl.BlockSpec(memory_space=pl.ANY)
    vmem = pl.BlockSpec(memory_space=pltpu.VMEM)
    back_rows = 2 * plan.lat_rim + 2 * plan.lon_rim + 4 * plan.corner
    square = (width, width)
    layer_out, grid_grad, mesh_grad = pl.pallas_call(
        functools.partial(layer_kernel, plan),
        out_shape=(
            jax.ShapeDtypeStruct((points, width), half),
            jax.ShapeDtypeStruct((points, width), half),
            jax.ShapeDtypeStruct((own, width), half),
        ),
        in_specs=[anywhere] * 9,
        out_specs=(vmem,) * 3,
        scratch_shapes=[
            pltpu.VMEM((points, width), half),
            pltpu.VMEM((points, width), half),
            pltpu.VMEM(edges.shape, jnp.int32),
            pltpu.VMEM(edges.shape, jnp.int32),
            pltpu.VMEM(square, half),
            pltpu.VMEM(square, half),
            pltpu.VMEM(square, half),
            pltpu.VMEM(square, half),
            pltpu.VMEM((nodes, width), half),
            pltpu.VMEM((2 * plan.lon_rim, width), half),
            pltpu.VMEM((plan.tiles, EDGE_SLOTS, plan.tile_points), jnp.int32),
            pltpu.VMEM((points, width), half),
            pltpu.VMEM((points, width), half),
            pltpu.VMEM((nodes, width), half),
            pltpu.VMEM((nodes, width), half),
            pltpu.VMEM((points, width), half),
            pltpu.VMEM((points, width), half),
            pltpu.VMEM((nodes, width), full),
            pltpu.VMEM((nodes, width), full),
            pltpu.VMEM((plan.keys, plan.tile_points), full),
            pltpu.VMEM((own, width), full),
            pltpu.VMEM((nodes, width), half),
            pltpu.VMEM((back_rows, width), half),
            pltpu.SemaphoreType.DMA((9,)),
            pltpu.SemaphoreType.DMA((8,)),
            pltpu.SemaphoreType.DMA((8,)),
            pltpu.SemaphoreType.DMA((8,)),
            pltpu.SemaphoreType.DMA((8,)),
        ],
        compiler_params=pltpu.CompilerParams(
            collective_id=0, has_side_effects=True, vmem_limit_bytes=52 * 2**20
        ),
        cost_estimate=pl.CostEstimate(
            flops=8 * points * width * width + 8 * nodes * width * width,
            bytes_accessed=8 * width * width + 8 * points * width,
            transcendentals=points * plan.keys * HEAD_COUNT,
        ),
    )(
        grid_feat.reshape(points, width), mesh_feat.reshape(own, width), edges, edge_mask,
        w_query, w_key, w_value, w_out, cotangent.reshape(points, width),
    )
    return (
        layer_out.reshape(grid_feat.shape),
        grid_grad.reshape(grid_feat.shape),
        mesh_grad.reshape(mesh_feat.shape),
    )


def solution(mesh):
    placed = (
        P("lat", "lon", None),
        P("lat", "lon", None),
        P(None, "lat", "lon"),
        P(None, "lat", "lon"),
        P(),
        P(),
        P(),
        P(),
        P("lat", "lon", None),
    )
    return jax.shard_map(
        local,
        mesh=mesh,
        in_specs=placed,
        out_specs=(P("lat", "lon", None), P("lat", "lon", None), P("lat", "lon", None)),
        check_vma=False,
    )
```

```python
import functools
import math

import jax
import jax.numpy as jnp
from jax import lax
from jax.experimental import pallas as pl
from jax.experimental.pallas import tpu as pltpu
from jax.sharding import PartitionSpec as P

HEAD_COUNT = 16
EDGE_SLOTS = 12
HALO_REACH = 4
TILE_MESH_ROWS = 2
ROW_GROUP = 16
NEG_FILL = -1e30

NN = (((1,), (0,)), ((), ()))
NT = (((1,), (1,)), ((), ()))
TN = (((0,), (0,)), ((), ()))


def mm(a, b, dims=NN):
    return lax.dot_general(a, b, dims, preferred_element_type=jnp.float32)


class Plan:
    def __init__(self, mesh_rows, mesh_cols, grid_rows, grid_cols, width, lat_count, lon_count):
        reach = HALO_REACH
        self.mesh_rows, self.mesh_cols = mesh_rows, mesh_cols
        self.grid_rows, self.grid_cols, self.width = grid_rows, grid_cols, width
        self.lat_count, self.lon_count = lat_count, lon_count
        self.head = width // HEAD_COUNT
        self.scale = 1.0 / math.sqrt(self.head)
        self.points = grid_rows * grid_cols
        self.own = mesh_rows * mesh_cols
        padded_rows = mesh_rows + 2 * reach
        self.mid = padded_rows * mesh_cols
        self.strip = padded_rows * reach
        self.nodes = self.mid + 2 * self.strip
        self.lat_rim = reach * mesh_cols
        self.lon_rim = mesh_rows * reach
        self.corner = reach * reach
        self.tiles = mesh_rows // TILE_MESH_ROWS
        self.tile_grid_rows = grid_rows // self.tiles
        self.tile_points = self.tile_grid_rows * grid_cols
        window_rows = TILE_MESH_ROWS + 2 * reach
        self.mid_step = TILE_MESH_ROWS * mesh_cols
        self.mid_keys = window_rows * mesh_cols
        self.side_step = TILE_MESH_ROWS * reach
        slack = max((tile * self.side_step) % ROW_GROUP for tile in range(self.tiles))
        covered = window_rows * reach + slack
        self.side_keys = min(self.strip, -(-covered // ROW_GROUP) * ROW_GROUP)
        self.keys = self.mid_keys + 2 * self.side_keys

    def side_start(self, tile):
        return (tile * self.side_step) // ROW_GROUP * ROW_GROUP

    def exchanges(self):
        mid, strip = self.mid, self.strip
        corner, lon_rim, lat_rim = self.corner, self.lon_rim, self.lat_rim
        left, right = mid, mid + strip
        return (
            (-1, 0, 0, lat_rim),
            (1, 0, mid - lat_rim, lat_rim),
            (0, -1, left + corner, lon_rim),
            (0, 1, right + corner, lon_rim),
            (-1, -1, left, corner),
            (1, -1, left + strip - corner, corner),
            (-1, 1, right, corner),
            (1, 1, right + strip - corner, corner),
        )


def pack_matrix(plan):
    rows = 2 * plan.lon_rim
    row = lax.broadcasted_iota(jnp.int32, (rows, plan.own), 0)
    node = lax.broadcasted_iota(jnp.int32, (rows, plan.own), 1)
    is_right = (row >= plan.lon_rim).astype(jnp.int32)
    within = row - is_right * plan.lon_rim
    mesh_row = within // HALO_REACH
    col = within - mesh_row * HALO_REACH + is_right * (plan.mesh_cols - HALO_REACH)
    hit = node == mesh_row * plan.mesh_cols + col
    return hit.astype(jnp.float32).astype(jnp.bfloat16)


def fill_slots(plan, lat_start, lon_start, edges_ref, mask_ref, slot_ref):
    reach, cols = HALO_REACH, plan.mesh_cols
    lon_total = plan.mesh_cols * plan.lon_count
    for tile in range(plan.tiles):
        rows = range(tile * plan.tile_grid_rows, (tile + 1) * plan.tile_grid_rows)
        target = jnp.concatenate([edges_ref[:, row, :] for row in rows], axis=1)
        live = jnp.concatenate([mask_ref[:, row, :] for row in rows], axis=1)
        if lon_total & (lon_total - 1):
            node_row = lax.div(target, jnp.full_like(target, lon_total))
        else:
            node_row = lax.shift_right_logical(
                target, jnp.full_like(target, lon_total.bit_length() - 1)
            )
        node_col = target - node_row * lon_total - lon_start + reach
        node_col = jnp.where(node_col < 0, node_col + lon_total, node_col)
        node_col = jnp.where(node_col >= lon_total, node_col - lon_total, node_col)
        node_row = node_row - lat_start + reach
        side = plan.mid_keys + node_row * reach - plan.side_start(tile)
        middle = node_row * cols + node_col - reach - tile * plan.mid_step
        right = side + plan.side_keys + node_col - cols - reach
        slot = jnp.where(
            node_col < reach, side + node_col, jnp.where(node_col < cols + reach, middle, right)
        )
        slot_ref[tile] = jnp.where(live > 0, slot, -1)


def attend_tiles(
    plan, slot_ref, q_ref, d_ref, k_ref, v_ref, att_ref, dq_ref, dk_ref, dv_ref, bias_ref
):
    head, tile_points = plan.head, plan.tile_points
    pair = 2 * head
    pairs = plan.width // pair
    low = (lax.broadcasted_iota(jnp.int32, (1, pair), 1) < head).astype(jnp.float32)
    high = (1.0 - low).astype(jnp.bfloat16)
    low = low.astype(jnp.bfloat16)
    dk_ref[...] = jnp.zeros_like(dk_ref)
    dv_ref[...] = jnp.zeros_like(dv_ref)

    def tile_step(tile, carry):
        rows = pl.ds(pl.multiple_of(tile * tile_points, tile_points), tile_points)
        side = plan.side_start(tile)
        windows = (
            (pl.ds(pl.multiple_of(tile * plan.mid_step, ROW_GROUP), plan.mid_keys), 0),
            (pl.ds(pl.multiple_of(plan.mid + side, ROW_GROUP), plan.side_keys), plan.mid_keys),
            (
                pl.ds(pl.multiple_of(plan.mid + plan.strip + side, ROW_GROUP), plan.side_keys),
                plan.mid_keys + plan.side_keys,
            ),
        )
        key_id = lax.broadcasted_iota(jnp.int32, (plan.keys, tile_points), 0)
        slots = slot_ref[tile]
        linked = key_id == slots[0:1]
        for slot in range(1, EDGE_SLOTS):
            linked = linked | (key_id == slots[slot : slot + 1])
        bias_ref[...] = jnp.where(linked, 0.0, NEG_FILL)

        def split(block):
            return jnp.concatenate([block * low, block * high], axis=0)

        def joined(both):
            kept = jnp.concatenate([both[:head, :tile_points], both[head:, tile_points:]], axis=0)
            return kept.astype(jnp.bfloat16).T

        def window_of(ref, lanes):
            return jnp.concatenate([ref[window, lanes] for window, _ in windows], axis=0)

        def add_window(ref, lanes, block):
            for window, first in windows:
                ref[window, lanes] += block[first : first + window.size]

        def first_products(index):
            lanes = slice(index * pair, (index + 1) * pair)
            q2 = split(q_ref[rows, lanes])
            d2 = split(d_ref[rows, lanes])
            k2 = window_of(k_ref, lanes)
            v2 = window_of(v_ref, lanes)
            return lanes, q2, d2, k2, v2, mm(k2, q2, NT), mm(v2, d2, NT)

        def rest(lanes, q2, d2, k2, v2, scores, d_prob):
            bias = bias_ref[...]
            scores = scores + jnp.concatenate([bias, bias], axis=1)
            exps = jnp.exp(scores - jnp.max(scores, axis=0, keepdims=True))
            prob = exps * (1.0 / jnp.sum(exps, axis=0, keepdims=True))
            half = prob.astype(jnp.bfloat16)
            centred = jnp.sum(prob * d_prob, axis=0, keepdims=True)
            d_score = (prob * (d_prob - centred)).astype(jnp.bfloat16)
            att_ref[rows, lanes] = joined(mm(v2, half, TN))
            dq_ref[rows, lanes] = joined(mm(k2, d_score, TN) * plan.scale)
            add_window(dk_ref, lanes, mm(d_score, q2))
            add_window(dv_ref, lanes, mm(half, d2))

        ready = first_products(0)
        for index in range(pairs):
            following = first_products(index + 1) if index + 1 < pairs else None
            rest(*ready)
            ready = following
        return carry

    lax.fori_loop(0, plan.tiles, tile_step, 0)


def column_tiles(width, body):
    tile = min(width, 512)

    def step(index, carry):
        body(pl.ds(pl.multiple_of(index * tile, tile), tile))
        return carry

    lax.fori_loop(0, width // tile, step, 0)


def layer_kernel(
    plan,
    grid_in, mesh_in, edges_in, mask_in, wq_in, wk_in, wv_in, wo_in, cot_in,
    out_hbm, grid_grad_hbm, mesh_grad_hbm,
    out_ref, grid_grad_ref, mesh_grad_ref, grid_ref, cot_ref, edges_ref, mask_ref, wq_ref, wk_ref, wv_ref, wo_ref,
    feat_ref, pack_ref, slot_ref, q_ref, d_ref, k_ref, v_ref, att_ref, dq_ref,
    dk_ref, dv_ref, bias_ref, own_ref, part_ref, back_ref,
    load_sem, store_sem, send_sem, recv_sem, back_send_sem, back_recv_sem,
):
    reach = HALO_REACH
    lat, lon = lax.axis_index("lat"), lax.axis_index("lon")
    exchanges = plan.exchanges()
    first_own = plan.lat_rim

    def device(lat_step, lon_step):
        return (
            lax.rem(lat + lat_step + plan.lat_count, plan.lat_count),
            lax.rem(lon + lon_step + plan.lon_count, plan.lon_count),
        )

    barrier = pltpu.get_barrier_semaphore()
    for lat_step, lon_step, _, _ in exchanges:
        pl.semaphore_signal(
            barrier, inc=1, device_id=device(lat_step, lon_step), device_id_type=pl.DeviceIdType.MESH
        )
    own_feat = feat_ref.at[pl.ds(first_own, plan.own)]
    loads = []
    for index, (source, target) in enumerate(
        (
            (mesh_in, own_feat), (edges_in, edges_ref), (mask_in, mask_ref), (grid_in, grid_ref),
            (wq_in, wq_ref), (cot_in, cot_ref), (wo_in, wo_ref), (wk_in, wk_ref), (wv_in, wv_ref),
        )
    ):
        load = pltpu.make_async_copy(source, target, load_sem.at[index])
        load.start()
        loads.append(load)
    mesh_load, edges_load, mask_load, grid_load, wq_load, cot_load, wo_load, wk_load, wv_load = loads

    mesh_load.wait()
    pack = pack_matrix(plan)
    pack_ref[...] = mm(pack, own_feat[...]).astype(jnp.bfloat16)
    edges_load.wait()
    mask_load.wait()
    fill_slots(
        plan, lat * plan.mesh_rows, lon * plan.mesh_cols, edges_ref, mask_ref, slot_ref
    )
    pl.semaphore_wait(barrier, len(exchanges))
    corner, lon_rim = plan.corner, plan.lon_rim
    sent = []
    for index, (lat_step, lon_step, first, count) in enumerate(exchanges):
        if lon_step == 0:
            start = first_own + (plan.own - count if lat_step < 0 else 0)
            source = feat_ref.at[pl.ds(start, count)]
        else:
            start = lon_rim if lon_step < 0 else 0
            if lat_step < 0:
                start += lon_rim - count
            source = pack_ref.at[pl.ds(start, count)]
        copy = pltpu.make_async_remote_copy(
            src_ref=source,
            dst_ref=feat_ref.at[pl.ds(first, count)],
            send_sem=send_sem.at[index],
            recv_sem=recv_sem.at[index],
            device_id=device(-lat_step, -lon_step),
            device_id_type=pl.DeviceIdType.MESH,
        )
        copy.start()
        sent.append(copy)

    grid_load.wait()
    wq_load.wait()

    def query_columns(columns):
        queries = mm(grid_ref[...], wq_ref[:, columns]).astype(jnp.bfloat16)
        q_ref[:, columns] = (queries.astype(jnp.float32) * plan.scale).astype(jnp.bfloat16)

    column_tiles(plan.width, query_columns)
    cot_load.wait()
    wo_load.wait()

    def d_columns(columns):
        d_ref[:, columns] = mm(cot_ref[...], wo_ref[columns, :], NT).astype(jnp.bfloat16)

    column_tiles(plan.width, d_columns)
    wk_load.wait()
    wv_load.wait()
    for copy in sent:
        copy.wait()

    def pair_columns(columns):
        feat = feat_ref[...]
        k_ref[:, columns] = mm(feat, wk_ref[:, columns]).astype(jnp.bfloat16)
        v_ref[:, columns] = mm(feat, wv_ref[:, columns]).astype(jnp.bfloat16)

    column_tiles(plan.width, pair_columns)
    attend_tiles(
        plan, slot_ref, q_ref, d_ref, k_ref, v_ref, att_ref, dq_ref, dk_ref, dv_ref, bias_ref
    )
    k_ref[...] = dk_ref[...].astype(jnp.bfloat16)
    v_ref[...] = dv_ref[...].astype(jnp.bfloat16)

    def part_columns(columns):
        part = mm(k_ref[...], wk_ref[columns, :], NT) + mm(v_ref[...], wv_ref[columns, :], NT)
        part_ref[:, columns] = part.astype(jnp.bfloat16)
        own_ref[:, columns] = part[first_own : first_own + plan.own]

    column_tiles(plan.width, part_columns)
    returned = []
    for index, (lat_step, lon_step, first, count) in enumerate(exchanges):
        if lon_step == 0:
            start = count if lat_step < 0 else 0
        else:
            base = 2 * plan.lat_rim
            if lat_step == 0:
                start = base + (lon_rim if lon_step < 0 else 0)
            else:
                base += 2 * lon_rim
                order = (0 if lon_step > 0 else 2) + (1 if lat_step < 0 else 0)
                start = base + order * corner
        copy = pltpu.make_async_remote_copy(
            src_ref=part_ref.at[pl.ds(first, count)],
            dst_ref=back_ref.at[pl.ds(start, count)],
            send_sem=back_send_sem.at[index],
            recv_sem=back_recv_sem.at[index],
            device_id=device(lat_step, lon_step),
            device_id_type=pl.DeviceIdType.MESH,
        )
        copy.start()
        returned.append(copy)

    def out_columns(columns):
        out = grid_ref[:, columns].astype(jnp.float32) + mm(att_ref[...], wo_ref[:, columns])
        out_ref[:, columns] = out.astype(jnp.bfloat16)
        grad = cot_ref[:, columns].astype(jnp.float32) + mm(dq_ref[...], wq_ref[columns, :], NT)
        grid_grad_ref[:, columns] = grad.astype(jnp.bfloat16)

    column_tiles(plan.width, out_columns)
    stores = [
        pltpu.make_async_copy(out_ref, out_hbm, store_sem.at[0]),
        pltpu.make_async_copy(grid_grad_ref, grid_grad_hbm, store_sem.at[1]),
        pltpu.make_async_copy(mesh_grad_ref, mesh_grad_hbm, store_sem.at[2]),
    ]
    stores[0].start()
    stores[1].start()
    for copy in returned:
        copy.wait()
    corners = [
        pack[0:corner], pack[lon_rim - corner : lon_rim],
        pack[lon_rim : lon_rim + corner], pack[2 * lon_rim - corner : 2 * lon_rim],
    ]
    unpack = jnp.concatenate([pack] + corners, axis=0)
    lat_terms = 2 * plan.lat_rim
    last_rim = pl.ds(plan.own - plan.lat_rim, plan.lat_rim)

    def mesh_columns(columns):
        total = own_ref[:, columns] + mm(unpack, back_ref[lat_terms:, columns], TN)
        own_ref[:, columns] = total
        for start, rows in ((0, pl.ds(0, plan.lat_rim)), (plan.lat_rim, last_rim)):
            own_ref[rows, columns] += back_ref[pl.ds(start, plan.lat_rim), columns].astype(
                jnp.float32
            )
        mesh_grad_ref[:, columns] = own_ref[:, columns].astype(jnp.bfloat16)

    column_tiles(plan.width, mesh_columns)
    stores[2].start()
    for store in stores:
        store.wait()


def store_kernel(out_in, grid_grad_in, mesh_grad_in, out_ref, grid_grad_ref, mesh_grad_ref, sem):
    copies = [
        pltpu.make_async_copy(source, target, sem.at[index])
        for index, (source, target) in enumerate(
            ((out_in, out_ref), (grid_grad_in, grid_grad_ref), (mesh_grad_in, mesh_grad_ref))
        )
    ]
    for copy in copies:
        copy.start()
    for copy in copies:
        copy.wait()


def local(grid_feat, mesh_feat, edges, edge_mask, w_query, w_key, w_value, w_out, cotangent):
    grid_rows, grid_cols, width = grid_feat.shape
    mesh_rows, mesh_cols, _ = mesh_feat.shape
    plan = Plan(
        mesh_rows, mesh_cols, grid_rows, grid_cols, width, lax.axis_size("lat"), lax.axis_size("lon")
    )
    half, full = jnp.bfloat16, jnp.float32
    points, own, nodes = plan.points, plan.own, plan.nodes
    anywhere = pl.BlockSpec(memory_space=pl.ANY)
    hbm = pl.BlockSpec(memory_space=pltpu.HBM)
    back_rows = 2 * plan.lat_rim + 2 * plan.lon_rim + 4 * plan.corner
    square = (width, width)
    layer_out, grid_grad, mesh_grad = pl.pallas_call(
        functools.partial(layer_kernel, plan),
        out_shape=(
            jax.ShapeDtypeStruct((points, width), half),
            jax.ShapeDtypeStruct((points, width), half),
            jax.ShapeDtypeStruct((own, width), half),
        ),
        in_specs=[hbm] * 9,
        out_specs=(hbm,) * 3,
        scratch_shapes=[
            pltpu.VMEM((points, width), half),
            pltpu.VMEM((points, width), half),
            pltpu.VMEM((own, width), half),
            pltpu.VMEM((points, width), half),
            pltpu.VMEM((points, width), half),
            pltpu.VMEM(edges.shape, jnp.int32),
            pltpu.VMEM(edges.shape, jnp.int32),
            pltpu.VMEM(square, half),
            pltpu.VMEM(square, half),
            pltpu.VMEM(square, half),
            pltpu.VMEM(square, half),
            pltpu.VMEM((nodes, width), half),
            pltpu.VMEM((2 * plan.lon_rim, width), half),
            pltpu.VMEM((plan.tiles, EDGE_SLOTS, plan.tile_points), jnp.int32),
            pltpu.VMEM((points, width), half),
            pltpu.VMEM((points, width), half),
            pltpu.VMEM((nodes, width), half),
            pltpu.VMEM((nodes, width), half),
            pltpu.VMEM((points, width), half),
            pltpu.VMEM((points, width), half),
            pltpu.VMEM((nodes, width), full),
            pltpu.VMEM((nodes, width), full),
            pltpu.VMEM((plan.keys, plan.tile_points), full),
            pltpu.VMEM((own, width), full),
            pltpu.VMEM((nodes, width), half),
            pltpu.VMEM((back_rows, width), half),
            pltpu.SemaphoreType.DMA((9,)),
            pltpu.SemaphoreType.DMA((3,)),
            pltpu.SemaphoreType.DMA((8,)),
            pltpu.SemaphoreType.DMA((8,)),
            pltpu.SemaphoreType.DMA((8,)),
            pltpu.SemaphoreType.DMA((8,)),
        ],
        compiler_params=pltpu.CompilerParams(
            collective_id=0, has_side_effects=True, vmem_limit_bytes=64 * 2**20
        ),
        cost_estimate=pl.CostEstimate(
            flops=8 * points * width * width + 8 * nodes * width * width,
            bytes_accessed=8 * width * width + 8 * points * width,
            transcendentals=points * plan.keys * HEAD_COUNT,
        ),
    )(
        grid_feat.reshape(points, width), mesh_feat.reshape(own, width), edges, edge_mask,
        w_query, w_key, w_value, w_out, cotangent.reshape(points, width),
    )
    results = (layer_out, grid_grad, mesh_grad)
    layer_out, grid_grad, mesh_grad = pl.pallas_call(
        store_kernel,
        out_shape=tuple(jax.ShapeDtypeStruct(x.shape, x.dtype) for x in results),
        in_specs=[anywhere] * 3,
        out_specs=(hbm,) * 3,
        scratch_shapes=[pltpu.SemaphoreType.DMA((3,))],
        compiler_params=pltpu.CompilerParams(vmem_limit_bytes=64 * 2**20),
    )(*results)
    return (
        layer_out.reshape(grid_feat.shape),
        grid_grad.reshape(grid_feat.shape),
        mesh_grad.reshape(mesh_feat.shape),
    )


def solution(mesh):
    placed = (
        P("lat", "lon", None),
        P("lat", "lon", None),
        P(None, "lat", "lon"),
        P(None, "lat", "lon"),
        P(),
        P(),
        P(),
        P(),
        P("lat", "lon", None),
    )
    return jax.shard_map(
        local,
        mesh=mesh,
        in_specs=placed,
        out_specs=(P("lat", "lon", None), P("lat", "lon", None), P("lat", "lon", None)),
        check_vma=False,
    )
```

```python
import functools
import math

import jax
import jax.numpy as jnp
from jax import lax
from jax.experimental import pallas as pl
from jax.experimental.pallas import tpu as pltpu
from jax.sharding import PartitionSpec as P

HEAD_COUNT = 16
EDGE_SLOTS = 12
HALO_REACH = 4
TILE_MESH_ROWS = 2
ROW_GROUP = 16
NEG_FILL = -1e30

NN = (((1,), (0,)), ((), ()))
NT = (((1,), (1,)), ((), ()))
TN = (((0,), (0,)), ((), ()))


def mm(a, b, dims=NN):
    return lax.dot_general(a, b, dims, preferred_element_type=jnp.float32)


class Plan:
    def __init__(self, mesh_rows, mesh_cols, grid_rows, grid_cols, width, lat_count, lon_count):
        reach = HALO_REACH
        self.mesh_rows, self.mesh_cols = mesh_rows, mesh_cols
        self.grid_rows, self.grid_cols, self.width = grid_rows, grid_cols, width
        self.lat_count, self.lon_count = lat_count, lon_count
        self.head = width // HEAD_COUNT
        self.scale = 1.0 / math.sqrt(self.head)
        self.points = grid_rows * grid_cols
        self.own = mesh_rows * mesh_cols
        padded_rows = mesh_rows + 2 * reach
        self.mid = padded_rows * mesh_cols
        self.strip = padded_rows * reach
        self.nodes = self.mid + 2 * self.strip
        self.lat_rim = reach * mesh_cols
        self.lon_rim = mesh_rows * reach
        self.corner = reach * reach
        self.tiles = mesh_rows // TILE_MESH_ROWS
        self.tile_grid_rows = grid_rows // self.tiles
        self.tile_points = self.tile_grid_rows * grid_cols
        window_rows = TILE_MESH_ROWS + 2 * reach
        self.mid_step = TILE_MESH_ROWS * mesh_cols
        self.mid_keys = window_rows * mesh_cols
        self.side_step = TILE_MESH_ROWS * reach
        slack = max((tile * self.side_step) % ROW_GROUP for tile in range(self.tiles))
        covered = window_rows * reach + slack
        self.side_keys = min(self.strip, -(-covered // ROW_GROUP) * ROW_GROUP)
        self.keys = self.mid_keys + 2 * self.side_keys

        self.early = (mesh_rows - reach) // TILE_MESH_ROWS

    def node_ranges(self, low, high):
        reach, cols = HALO_REACH, self.mesh_cols
        right = self.mid + self.strip
        return (
            slice(low * cols, high * cols),
            slice(self.mid + low * reach, self.mid + high * reach),
            slice(right + low * reach, right + high * reach),
        )

    def side_start(self, tile):
        return (tile * self.side_step) // ROW_GROUP * ROW_GROUP

    def exchanges(self):
        mid, strip = self.mid, self.strip
        corner, lon_rim, lat_rim = self.corner, self.lon_rim, self.lat_rim
        left, right = mid, mid + strip
        return (
            (-1, 0, 0, lat_rim),
            (-1, -1, left, corner),
            (-1, 1, right, corner),
            (0, -1, left + corner, lon_rim),
            (0, 1, right + corner, lon_rim),
            (1, 0, mid - lat_rim, lat_rim),
            (1, -1, left + strip - corner, corner),
            (1, 1, right + strip - corner, corner),
        )


def pack_matrix(plan):
    rows = 2 * plan.lon_rim
    row = lax.broadcasted_iota(jnp.int32, (rows, plan.own), 0)
    node = lax.broadcasted_iota(jnp.int32, (rows, plan.own), 1)
    is_right = (row >= plan.lon_rim).astype(jnp.int32)
    within = row - is_right * plan.lon_rim
    mesh_row = within // HALO_REACH
    col = within - mesh_row * HALO_REACH + is_right * (plan.mesh_cols - HALO_REACH)
    hit = node == mesh_row * plan.mesh_cols + col
    return hit.astype(jnp.float32).astype(jnp.bfloat16)


def fill_slots(plan, lat_start, lon_start, edges_ref, mask_ref, slot_ref):
    reach, cols = HALO_REACH, plan.mesh_cols
    lon_total = plan.mesh_cols * plan.lon_count
    for tile in range(plan.tiles):
        rows = range(tile * plan.tile_grid_rows, (tile + 1) * plan.tile_grid_rows)
        target = jnp.concatenate([edges_ref[:, row, :] for row in rows], axis=1)
        live = jnp.concatenate([mask_ref[:, row, :] for row in rows], axis=1)
        if lon_total & (lon_total - 1):
            node_row = lax.div(target, jnp.full_like(target, lon_total))
        else:
            node_row = lax.shift_right_logical(
                target, jnp.full_like(target, lon_total.bit_length() - 1)
            )
        node_col = target - node_row * lon_total - lon_start + reach
        node_col = jnp.where(node_col < 0, node_col + lon_total, node_col)
        node_col = jnp.where(node_col >= lon_total, node_col - lon_total, node_col)
        node_row = node_row - lat_start + reach
        side = plan.mid_keys + node_row * reach - plan.side_start(tile)
        middle = node_row * cols + node_col - reach - tile * plan.mid_step
        right = side + plan.side_keys + node_col - cols - reach
        slot = jnp.where(
            node_col < reach, side + node_col, jnp.where(node_col < cols + reach, middle, right)
        )
        slot_ref[tile] = jnp.where(live > 0, slot, -1)


def attend_tiles(
    plan, slot_ref, q_ref, d_ref, k_ref, v_ref, att_ref, dq_ref, dk_ref, dv_ref, bias_ref,
    at_middle,
):
    head, tile_points = plan.head, plan.tile_points
    pair = 2 * head
    pairs = plan.width // pair
    low = (lax.broadcasted_iota(jnp.int32, (1, pair), 1) < head).astype(jnp.float32)
    high = (1.0 - low).astype(jnp.bfloat16)
    low = low.astype(jnp.bfloat16)
    dk_ref[...] = jnp.zeros_like(dk_ref)
    dv_ref[...] = jnp.zeros_like(dv_ref)

    def tile_step(tile, carry):
        pl.when(tile == plan.early)(at_middle)
        rows = pl.ds(pl.multiple_of(tile * tile_points, tile_points), tile_points)
        side = plan.side_start(tile)
        windows = (
            (pl.ds(pl.multiple_of(tile * plan.mid_step, ROW_GROUP), plan.mid_keys), 0),
            (pl.ds(pl.multiple_of(plan.mid + side, ROW_GROUP), plan.side_keys), plan.mid_keys),
            (
                pl.ds(pl.multiple_of(plan.mid + plan.strip + side, ROW_GROUP), plan.side_keys),
                plan.mid_keys + plan.side_keys,
            ),
        )
        key_id = lax.broadcasted_iota(jnp.int32, (plan.keys, tile_points), 0)
        slots = slot_ref[tile]
        linked = key_id == slots[0:1]
        for slot in range(1, EDGE_SLOTS):
            linked = linked | (key_id == slots[slot : slot + 1])
        bias_ref[...] = jnp.where(linked, 0.0, NEG_FILL)

        def split(block):
            return jnp.concatenate([block * low, block * high], axis=0)

        def joined(both):
            kept = jnp.concatenate([both[:head, :tile_points], both[head:, tile_points:]], axis=0)
            return kept.astype(jnp.bfloat16).T

        def window_of(ref, lanes):
            return jnp.concatenate([ref[window, lanes] for window, _ in windows], axis=0)

        def add_window(ref, lanes, block):
            for window, first in windows:
                ref[window, lanes] += block[first : first + window.size]

        def first_products(index):
            lanes = slice(index * pair, (index + 1) * pair)
            q2 = split(q_ref[rows, lanes])
            d2 = split(d_ref[rows, lanes])
            k2 = window_of(k_ref, lanes)
            v2 = window_of(v_ref, lanes)
            return lanes, q2, d2, k2, v2, mm(k2, q2, NT), mm(v2, d2, NT)

        def rest(lanes, q2, d2, k2, v2, scores, d_prob):
            bias = bias_ref[...]
            scores = scores + jnp.concatenate([bias, bias], axis=1)
            exps = jnp.exp(scores - jnp.max(scores, axis=0, keepdims=True))
            prob = exps * (1.0 / jnp.sum(exps, axis=0, keepdims=True))
            half = prob.astype(jnp.bfloat16)
            centred = jnp.sum(prob * d_prob, axis=0, keepdims=True)
            d_score = (prob * (d_prob - centred)).astype(jnp.bfloat16)
            att_ref[rows, lanes] = joined(mm(v2, half, TN))
            dq_ref[rows, lanes] = joined(mm(k2, d_score, TN) * plan.scale)
            add_window(dk_ref, lanes, mm(d_score, q2))
            add_window(dv_ref, lanes, mm(half, d2))

        ready = first_products(0)
        for index in range(pairs):
            following = first_products(index + 1) if index + 1 < pairs else None
            rest(*ready)
            ready = following
        return carry

    lax.fori_loop(0, plan.tiles, tile_step, 0)


def column_tiles(width, body):
    tile = min(width, 512)

    def step(index, carry):
        body(pl.ds(pl.multiple_of(index * tile, tile), tile))
        return carry

    lax.fori_loop(0, width // tile, step, 0)


def layer_kernel(
    plan,
    grid_in, mesh_in, edges_in, mask_in, wq_in, wk_in, wv_in, wo_in, cot_in,
    out_hbm, grid_grad_hbm, mesh_grad_hbm,
    out_ref, grid_grad_ref, mesh_grad_ref, grid_ref, cot_ref, edges_ref, mask_ref, wq_ref, wk_ref, wv_ref, wo_ref,
    feat_ref, pack_ref, slot_ref, q_ref, d_ref, k_ref, v_ref, att_ref, dq_ref,
    dk_ref, dv_ref, dk_half_ref, dv_half_ref, bias_ref, own_ref, part_ref, back_ref,
    load_sem, store_sem, send_sem, recv_sem, back_send_sem, back_recv_sem,
):
    reach = HALO_REACH
    lat, lon = lax.axis_index("lat"), lax.axis_index("lon")
    exchanges = plan.exchanges()
    first_own = plan.lat_rim

    def device(lat_step, lon_step):
        return (
            lax.rem(lat + lat_step + plan.lat_count, plan.lat_count),
            lax.rem(lon + lon_step + plan.lon_count, plan.lon_count),
        )

    barrier = pltpu.get_barrier_semaphore()
    for lat_step, lon_step, _, _ in exchanges:
        pl.semaphore_signal(
            barrier, inc=1, device_id=device(lat_step, lon_step), device_id_type=pl.DeviceIdType.MESH
        )
    own_feat = feat_ref.at[pl.ds(first_own, plan.own)]
    loads = []
    for index, (source, target) in enumerate(
        (
            (mesh_in, own_feat), (edges_in, edges_ref), (mask_in, mask_ref), (grid_in, grid_ref),
            (wq_in, wq_ref), (cot_in, cot_ref), (wo_in, wo_ref), (wk_in, wk_ref), (wv_in, wv_ref),
        )
    ):
        load = pltpu.make_async_copy(source, target, load_sem.at[index])
        load.start()
        loads.append(load)
    mesh_load, edges_load, mask_load, grid_load, wq_load, cot_load, wo_load, wk_load, wv_load = loads

    mesh_load.wait()
    pack = pack_matrix(plan)
    pack_ref[...] = mm(pack, own_feat[...]).astype(jnp.bfloat16)
    edges_load.wait()
    mask_load.wait()
    fill_slots(
        plan, lat * plan.mesh_rows, lon * plan.mesh_cols, edges_ref, mask_ref, slot_ref
    )
    pl.semaphore_wait(barrier, len(exchanges))
    corner, lon_rim = plan.corner, plan.lon_rim
    sent = []
    for index, (lat_step, lon_step, first, count) in enumerate(exchanges):
        if lon_step == 0:
            start = first_own + (plan.own - count if lat_step < 0 else 0)
            source = feat_ref.at[pl.ds(start, count)]
        else:
            start = lon_rim if lon_step < 0 else 0
            if lat_step < 0:
                start += lon_rim - count
            source = pack_ref.at[pl.ds(start, count)]
        copy = pltpu.make_async_remote_copy(
            src_ref=source,
            dst_ref=feat_ref.at[pl.ds(first, count)],
            send_sem=send_sem.at[index],
            recv_sem=recv_sem.at[index],
            device_id=device(-lat_step, -lon_step),
            device_id_type=pl.DeviceIdType.MESH,
        )
        sent.append(copy)
    above, beside, below = sent[:3], sent[3:5], sent[5:]
    for copy in above + beside:
        copy.start()

    grid_load.wait()
    wq_load.wait()

    def query_columns(columns):
        queries = mm(grid_ref[...], wq_ref[:, columns]).astype(jnp.bfloat16)
        q_ref[:, columns] = (queries.astype(jnp.float32) * plan.scale).astype(jnp.bfloat16)

    column_tiles(plan.width, query_columns)
    cot_load.wait()
    wo_load.wait()

    def d_columns(columns):
        d_ref[:, columns] = mm(cot_ref[...], wo_ref[columns, :], NT).astype(jnp.bfloat16)

    column_tiles(plan.width, d_columns)
    wk_load.wait()
    wv_load.wait()
    for copy in below:
        copy.start()

    def project(low, high):
        ranges = plan.node_ranges(low, high)

        def pair_columns(columns):
            feat = jnp.concatenate([feat_ref[nodes, :] for nodes in ranges], axis=0)
            for weight_ref, target_ref in ((wk_ref, k_ref), (wv_ref, v_ref)):
                rows = mm(feat, weight_ref[:, columns]).astype(jnp.bfloat16)
                first = 0
                for nodes in ranges:
                    count = nodes.stop - nodes.start
                    target_ref[nodes, columns] = rows[first : first + count]
                    first += count

        column_tiles(plan.width, pair_columns)

    def project_gradients(low, high):
        ranges = plan.node_ranges(low, high)
        for nodes in ranges:
            dk_half_ref[nodes, :] = dk_ref[nodes, :].astype(jnp.bfloat16)
            dv_half_ref[nodes, :] = dv_ref[nodes, :].astype(jnp.bfloat16)

        def part_columns(columns):
            d_keys = jnp.concatenate([dk_half_ref[nodes, :] for nodes in ranges], axis=0)
            d_values = jnp.concatenate([dv_half_ref[nodes, :] for nodes in ranges], axis=0)
            part = mm(d_keys, wk_ref[columns, :], NT) + mm(d_values, wv_ref[columns, :], NT)
            if low > 0:
                own_ref[:, columns] = part[: plan.own]
            part = part.astype(jnp.bfloat16)
            first = 0
            for nodes in ranges:
                count = nodes.stop - nodes.start
                part_ref[nodes, columns] = part[first : first + count]
                first += count

        column_tiles(plan.width, part_columns)

    returned = []
    for index, (lat_step, lon_step, first, count) in enumerate(exchanges):
        if lon_step == 0:
            start = count if lat_step < 0 else 0
        else:
            base = 2 * plan.lat_rim
            if lat_step == 0:
                start = base + (lon_rim if lon_step < 0 else 0)
            else:
                base += 2 * lon_rim
                order = (0 if lon_step > 0 else 2) + (1 if lat_step < 0 else 0)
                start = base + order * corner
        copy = pltpu.make_async_remote_copy(
            src_ref=part_ref.at[pl.ds(first, count)],
            dst_ref=back_ref.at[pl.ds(start, count)],
            send_sem=back_send_sem.at[index],
            recv_sem=back_recv_sem.at[index],
            device_id=device(lat_step, lon_step),
            device_id_type=pl.DeviceIdType.MESH,
        )
        returned.append(copy)

    padded_rows = plan.mesh_rows + 2 * reach

    def at_middle():
        for copy in below:
            copy.wait()
        project(plan.mesh_rows + reach, padded_rows)
        project_gradients(0, reach)
        for copy in returned[:3]:
            copy.start()

    for copy in above + beside:
        copy.wait()
    project(0, plan.mesh_rows + reach)
    attend_tiles(
        plan, slot_ref, q_ref, d_ref, k_ref, v_ref, att_ref, dq_ref, dk_ref, dv_ref, bias_ref,
        at_middle,
    )
    project_gradients(reach, padded_rows)
    for copy in returned[3:]:
        copy.start()

    def out_columns(columns):
        out = grid_ref[:, columns].astype(jnp.float32) + mm(att_ref[...], wo_ref[:, columns])
        out_ref[:, columns] = out.astype(jnp.bfloat16)
        grad = cot_ref[:, columns].astype(jnp.float32) + mm(dq_ref[...], wq_ref[columns, :], NT)
        grid_grad_ref[:, columns] = grad.astype(jnp.bfloat16)

    column_tiles(plan.width, out_columns)
    stores = [
        pltpu.make_async_copy(out_ref, out_hbm, store_sem.at[0]),
        pltpu.make_async_copy(grid_grad_ref, grid_grad_hbm, store_sem.at[1]),
        pltpu.make_async_copy(mesh_grad_ref, mesh_grad_hbm, store_sem.at[2]),
    ]
    stores[0].start()
    stores[1].start()
    for copy in returned:
        copy.wait()
    corners = [
        pack[0:corner], pack[lon_rim - corner : lon_rim],
        pack[lon_rim : lon_rim + corner], pack[2 * lon_rim - corner : 2 * lon_rim],
    ]
    unpack = jnp.concatenate([pack] + corners, axis=0)
    lat_terms = 2 * plan.lat_rim
    last_rim = pl.ds(plan.own - plan.lat_rim, plan.lat_rim)

    def mesh_columns(columns):
        total = own_ref[:, columns] + mm(unpack, back_ref[lat_terms:, columns], TN)
        own_ref[:, columns] = total
        for start, rows in ((0, pl.ds(0, plan.lat_rim)), (plan.lat_rim, last_rim)):
            own_ref[rows, columns] += back_ref[pl.ds(start, plan.lat_rim), columns].astype(
                jnp.float32
            )
        mesh_grad_ref[:, columns] = own_ref[:, columns].astype(jnp.bfloat16)

    column_tiles(plan.width, mesh_columns)
    stores[2].start()
    for store in stores:
        store.wait()


def store_kernel(rows, *refs):
    sources, targets, held = refs[:3], refs[3:6], refs[6:9]
    load_sem, store_sem = refs[9:]
    loads, stores = [], []
    for source, target, buffer in zip(sources, targets, held):
        for start in range(0, source.shape[0], rows):
            part = pl.ds(start, rows)
            index = len(loads)
            loads.append(
                pltpu.make_async_copy(source.at[part], buffer.at[part], load_sem.at[index])
            )
            stores.append(
                pltpu.make_async_copy(buffer.at[part], target.at[part], store_sem.at[index])
            )
    for load in loads:
        load.start()
    for load, store in zip(loads, stores):
        load.wait()
        store.start()
    for store in stores:
        store.wait()


def local(grid_feat, mesh_feat, edges, edge_mask, w_query, w_key, w_value, w_out, cotangent):
    grid_rows, grid_cols, width = grid_feat.shape
    mesh_rows, mesh_cols, _ = mesh_feat.shape
    plan = Plan(
        mesh_rows, mesh_cols, grid_rows, grid_cols, width, lax.axis_size("lat"), lax.axis_size("lon")
    )
    half, full = jnp.bfloat16, jnp.float32
    points, own, nodes = plan.points, plan.own, plan.nodes
    anywhere = pl.BlockSpec(memory_space=pl.ANY)
    hbm = pl.BlockSpec(memory_space=pltpu.HBM)
    back_rows = 2 * plan.lat_rim + 2 * plan.lon_rim + 4 * plan.corner
    square = (width, width)
    layer_out, grid_grad, mesh_grad = pl.pallas_call(
        functools.partial(layer_kernel, plan),
        out_shape=(
            jax.ShapeDtypeStruct((points, width), half),
            jax.ShapeDtypeStruct((points, width), half),
            jax.ShapeDtypeStruct((own, width), half),
        ),
        in_specs=[hbm] * 9,
        out_specs=(hbm,) * 3,
        scratch_shapes=[
            pltpu.VMEM((points, width), half),
            pltpu.VMEM((points, width), half),
            pltpu.VMEM((own, width), half),
            pltpu.VMEM((points, width), half),
            pltpu.VMEM((points, width), half),
            pltpu.VMEM(edges.shape, jnp.int32),
            pltpu.VMEM(edges.shape, jnp.int32),
            pltpu.VMEM(square, half),
            pltpu.VMEM(square, half),
            pltpu.VMEM(square, half),
            pltpu.VMEM(square, half),
            pltpu.VMEM((nodes, width), half),
            pltpu.VMEM((2 * plan.lon_rim, width), half),
            pltpu.VMEM((plan.tiles, EDGE_SLOTS, plan.tile_points), jnp.int32),
            pltpu.VMEM((points, width), half),
            pltpu.VMEM((points, width), half),
            pltpu.VMEM((nodes, width), half),
            pltpu.VMEM((nodes, width), half),
            pltpu.VMEM((points, width), half),
            pltpu.VMEM((points, width), half),
            pltpu.VMEM((nodes, width), full),
            pltpu.VMEM((nodes, width), full),
            pltpu.VMEM((nodes, width), half),
            pltpu.VMEM((nodes, width), half),
            pltpu.VMEM((plan.keys, plan.tile_points), full),
            pltpu.VMEM((own, width), full),
            pltpu.VMEM((nodes, width), half),
            pltpu.VMEM((back_rows, width), half),
            pltpu.SemaphoreType.DMA((9,)),
            pltpu.SemaphoreType.DMA((3,)),
            pltpu.SemaphoreType.DMA((8,)),
            pltpu.SemaphoreType.DMA((8,)),
            pltpu.SemaphoreType.DMA((8,)),
            pltpu.SemaphoreType.DMA((8,)),
        ],
        compiler_params=pltpu.CompilerParams(
            collective_id=0, has_side_effects=True, vmem_limit_bytes=64 * 2**20
        ),
        cost_estimate=pl.CostEstimate(
            flops=8 * points * width * width + 8 * nodes * width * width,
            bytes_accessed=8 * width * width + 8 * points * width,
            transcendentals=points * plan.keys * HEAD_COUNT,
        ),
    )(
        grid_feat.reshape(points, width), mesh_feat.reshape(own, width), edges, edge_mask,
        w_query, w_key, w_value, w_out, cotangent.reshape(points, width),
    )
    results = (layer_out, grid_grad, mesh_grad)
    layer_out, grid_grad, mesh_grad = pl.pallas_call(
        functools.partial(store_kernel, own),
        out_shape=tuple(jax.ShapeDtypeStruct(x.shape, x.dtype) for x in results),
        in_specs=[anywhere] * 3,
        out_specs=(hbm,) * 3,
        scratch_shapes=[pltpu.VMEM(x.shape, x.dtype) for x in results]
        + [pltpu.SemaphoreType.DMA((2 * points // own + 1,))] * 2,
        compiler_params=pltpu.CompilerParams(vmem_limit_bytes=64 * 2**20),
    )(*results)
    return (
        layer_out.reshape(grid_feat.shape),
        grid_grad.reshape(grid_feat.shape),
        mesh_grad.reshape(mesh_feat.shape),
    )


def solution(mesh):
    placed = (
        P("lat", "lon", None),
        P("lat", "lon", None),
        P(None, "lat", "lon"),
        P(None, "lat", "lon"),
        P(),
        P(),
        P(),
        P(),
        P("lat", "lon", None),
    )
    return jax.shard_map(
        local,
        mesh=mesh,
        in_specs=placed,
        out_specs=(P("lat", "lon", None), P("lat", "lon", None), P("lat", "lon", None)),
        check_vma=False,
    )
```

```python
import functools
import math

import jax
import jax.numpy as jnp
from jax import lax
from jax.experimental import pallas as pl
from jax.experimental.pallas import tpu as pltpu
from jax.sharding import PartitionSpec as P

HEAD_COUNT = 16
EDGE_SLOTS = 12
HALO_REACH = 4
TILE_MESH_ROWS = 4
ROW_GROUP = 16
NEG_FILL = -1e30

NN = (((1,), (0,)), ((), ()))
NT = (((1,), (1,)), ((), ()))
TN = (((0,), (0,)), ((), ()))


def mm(a, b, dims=NN):
    return lax.dot_general(a, b, dims, preferred_element_type=jnp.float32)


class Plan:
    def __init__(self, mesh_rows, mesh_cols, grid_rows, grid_cols, width, lat_count, lon_count):
        reach = HALO_REACH
        self.mesh_rows, self.mesh_cols = mesh_rows, mesh_cols
        self.grid_rows, self.grid_cols, self.width = grid_rows, grid_cols, width
        self.lat_count, self.lon_count = lat_count, lon_count
        self.head = width // HEAD_COUNT
        self.scale = 1.0 / math.sqrt(self.head)
        self.points = grid_rows * grid_cols
        self.own = mesh_rows * mesh_cols
        padded_rows = mesh_rows + 2 * reach
        self.mid = padded_rows * mesh_cols
        self.strip = padded_rows * reach
        self.nodes = self.mid + 2 * self.strip
        self.lat_rim = reach * mesh_cols
        self.lon_rim = mesh_rows * reach
        self.corner = reach * reach
        self.block_cols = 2 * reach
        self.blocks = (mesh_cols + 2 * reach) // self.block_cols
        self.block = padded_rows * self.block_cols
        self.col_tiles = mesh_cols // self.block_cols
        self.row_tiles = mesh_rows // TILE_MESH_ROWS
        self.tiles = self.row_tiles * self.col_tiles
        self.tile_grid_rows = grid_rows // self.row_tiles
        self.tile_grid_cols = grid_cols // self.col_tiles
        self.tile_points = self.tile_grid_rows * self.tile_grid_cols
        self.row_step = TILE_MESH_ROWS * self.block_cols
        self.side_keys = (TILE_MESH_ROWS + 2 * reach) * self.block_cols
        self.keys = 2 * self.side_keys
        self.early = (mesh_rows - reach) // TILE_MESH_ROWS * self.col_tiles

    def node_ranges(self, low, high):
        reach, cols = HALO_REACH, self.mesh_cols
        right = self.mid + self.strip
        return (
            slice(low * cols, high * cols),
            slice(self.mid + low * reach, self.mid + high * reach),
            slice(right + low * reach, right + high * reach),
        )

    def block_ranges(self, low, high):
        return tuple(
            slice(
                block * self.block + low * self.block_cols,
                block * self.block + high * self.block_cols,
            )
            for block in range(self.blocks)
        )

    def exchanges(self):
        mid, strip = self.mid, self.strip
        corner, lon_rim, lat_rim = self.corner, self.lon_rim, self.lat_rim
        left, right = mid, mid + strip
        return (
            (-1, 0, 0, lat_rim),
            (-1, -1, left, corner),
            (-1, 1, right, corner),
            (0, -1, left + corner, lon_rim),
            (0, 1, right + corner, lon_rim),
            (1, 0, mid - lat_rim, lat_rim),
            (1, -1, left + strip - corner, corner),
            (1, 1, right + strip - corner, corner),
        )


def pack_matrix(plan):
    rows = 2 * plan.lon_rim
    row = lax.broadcasted_iota(jnp.int32, (rows, plan.own), 0)
    node = lax.broadcasted_iota(jnp.int32, (rows, plan.own), 1)
    is_right = (row >= plan.lon_rim).astype(jnp.int32)
    within = row - is_right * plan.lon_rim
    mesh_row = within // HALO_REACH
    col = within - mesh_row * HALO_REACH + is_right * (plan.mesh_cols - HALO_REACH)
    hit = node == mesh_row * plan.mesh_cols + col
    return hit.astype(jnp.float32).astype(jnp.bfloat16)


def block_permutation(plan, rows, to_blocks):
    reach, cols, wide = HALO_REACH, plan.mesh_cols, plan.block_cols
    count = rows * (cols + 2 * reach)
    vector = (count, 1) if to_blocks else (1, count)
    node = lax.broadcasted_iota(jnp.int32, vector, 0 if to_blocks else 1)
    block = jnp.zeros_like(node)
    for edge in range(1, plan.blocks):
        block = block + (node >= edge * rows * wide).astype(jnp.int32)
    within = node - block * (rows * wide)
    row = within // wide
    col = within - row * wide + block * wide
    left = rows * cols + row * reach + col
    middle = row * cols + col - reach
    right = left + rows * reach - reach - cols
    place = jnp.where(col < reach, left, jnp.where(col < reach + cols, middle, right))
    other = lax.broadcasted_iota(jnp.int32, (count, count), 1 if to_blocks else 0)
    return (other == place).astype(jnp.float32).astype(jnp.bfloat16)


def fill_slots(plan, lat_start, lon_start, edges_ref, mask_ref, slot_ref):
    reach, wide = HALO_REACH, plan.block_cols
    lon_total = plan.mesh_cols * plan.lon_count
    for tile in range(plan.tiles):
        row_tile, col_tile = divmod(tile, plan.col_tiles)
        rows = range(row_tile * plan.tile_grid_rows, (row_tile + 1) * plan.tile_grid_rows)
        cols = slice(col_tile * plan.tile_grid_cols, (col_tile + 1) * plan.tile_grid_cols)
        target = jnp.concatenate([edges_ref[:, row, cols] for row in rows], axis=1)
        live = jnp.concatenate([mask_ref[:, row, cols] for row in rows], axis=1)
        if lon_total & (lon_total - 1):
            node_row = lax.div(target, jnp.full_like(target, lon_total))
        else:
            node_row = lax.shift_right_logical(
                target, jnp.full_like(target, lon_total.bit_length() - 1)
            )
        node_col = target - node_row * lon_total - lon_start + reach
        node_col = jnp.where(node_col < 0, node_col + lon_total, node_col)
        node_col = jnp.where(node_col >= lon_total, node_col - lon_total, node_col)
        node_row = node_row - lat_start + reach - row_tile * TILE_MESH_ROWS
        node_col = node_col - col_tile * wide
        first = node_row * wide + node_col
        slot = jnp.where(node_col < wide, first, first + (plan.side_keys - wide))
        slot_ref[tile] = jnp.where(live > 0, slot, -1)


def attend_tiles(
    plan, slot_ref, q_ref, d_ref, k_ref, v_ref, att_ref, dq_ref, dk_ref, dv_ref, bias_ref,
    at_middle,
):
    head, tile_points = plan.head, plan.tile_points
    pair = 2 * head
    pairs = plan.width // pair
    low = (lax.broadcasted_iota(jnp.int32, (1, pair), 1) < head).astype(jnp.float32)
    high = (1.0 - low).astype(jnp.bfloat16)
    low = low.astype(jnp.bfloat16)
    dk_ref[...] = jnp.zeros_like(dk_ref)
    dv_ref[...] = jnp.zeros_like(dv_ref)

    def tile_step(tile, carry):
        pl.when(tile == plan.early)(at_middle)
        row_tile, col_tile = tile // plan.col_tiles, tile % plan.col_tiles
        first_point = (
            row_tile * (plan.tile_grid_rows * plan.grid_cols) + col_tile * plan.tile_grid_cols
        )
        segments = tuple(
            pl.ds(
                pl.multiple_of(first_point + row * plan.grid_cols, ROW_GROUP), plan.tile_grid_cols
            )
            for row in range(plan.tile_grid_rows)
        )
        first_key = col_tile * plan.block + row_tile * plan.row_step
        windows = tuple(
            (
                pl.ds(pl.multiple_of(first_key + side * plan.block, ROW_GROUP), plan.side_keys),
                side * plan.side_keys,
            )
            for side in range(2)
        )
        key_id = lax.broadcasted_iota(jnp.int32, (plan.keys, tile_points), 0)
        slots = slot_ref[tile]
        linked = key_id == slots[0:1]
        for slot in range(1, EDGE_SLOTS):
            linked = linked | (key_id == slots[slot : slot + 1])
        bias_ref[...] = jnp.where(linked, 0.0, NEG_FILL)

        def split(block):
            return jnp.concatenate([block * low, block * high], axis=0)

        def joined(both):
            kept = jnp.concatenate([both[:head, :tile_points], both[head:, tile_points:]], axis=0)
            return kept.astype(jnp.bfloat16).T

        def points_of(ref, lanes):
            return jnp.concatenate([ref[segment, lanes] for segment in segments], axis=0)

        def put_points(ref, lanes, block):
            wide = plan.tile_grid_cols
            for row, segment in enumerate(segments):
                ref[segment, lanes] = block[row * wide : (row + 1) * wide]

        def window_of(ref, lanes):
            return jnp.concatenate([ref[window, lanes] for window, _ in windows], axis=0)

        def add_window(ref, lanes, block):
            for window, first in windows:
                ref[window, lanes] += block[first : first + window.size]

        def first_products(index):
            lanes = slice(index * pair, (index + 1) * pair)
            q2 = split(points_of(q_ref, lanes))
            d2 = split(points_of(d_ref, lanes))
            k2 = window_of(k_ref, lanes)
            v2 = window_of(v_ref, lanes)
            return lanes, q2, d2, k2, v2, mm(k2, q2, NT), mm(v2, d2, NT)

        def rest(lanes, q2, d2, k2, v2, scores, d_prob):
            bias = bias_ref[...]
            scores = scores + jnp.concatenate([bias, bias], axis=1)
            exps = jnp.exp(scores - jnp.max(scores, axis=0, keepdims=True))
            prob = exps * (1.0 / jnp.sum(exps, axis=0, keepdims=True))
            half = prob.astype(jnp.bfloat16)
            centred = jnp.sum(prob * d_prob, axis=0, keepdims=True)
            d_score = (prob * (d_prob - centred)).astype(jnp.bfloat16)
            put_points(att_ref, lanes, joined(mm(v2, half, TN)))
            put_points(dq_ref, lanes, joined(mm(k2, d_score, TN) * plan.scale))
            add_window(dk_ref, lanes, mm(d_score, q2))
            add_window(dv_ref, lanes, mm(half, d2))

        ready = first_products(0)
        for index in range(pairs):
            following = first_products(index + 1) if index + 1 < pairs else None
            rest(*ready)
            ready = following
        return carry

    lax.fori_loop(0, plan.tiles, tile_step, 0)


def column_tiles(width, body):
    tile = min(width, 512)

    def step(index, carry):
        body(pl.ds(pl.multiple_of(index * tile, tile), tile))
        return carry

    lax.fori_loop(0, width // tile, step, 0)


def layer_kernel(
    plan,
    grid_in, mesh_in, edges_in, mask_in, wq_in, wk_in, wv_in, wo_in, cot_in,
    out_hbm, grid_grad_hbm, mesh_grad_hbm,
    out_ref, grid_grad_ref, mesh_grad_ref, grid_ref, cot_ref, edges_ref, mask_ref, wq_ref, wk_ref, wv_ref, wo_ref,
    feat_ref, pack_ref, slot_ref, q_ref, d_ref, k_ref, v_ref, att_ref, dq_ref,
    dk_ref, dv_ref, dk_half_ref, dv_half_ref, bias_ref, own_ref, part_ref, back_ref,
    load_sem, store_sem, send_sem, recv_sem, back_send_sem, back_recv_sem,
):
    reach = HALO_REACH
    lat, lon = lax.axis_index("lat"), lax.axis_index("lon")
    exchanges = plan.exchanges()
    first_own = plan.lat_rim

    def device(lat_step, lon_step):
        return (
            lax.rem(lat + lat_step + plan.lat_count, plan.lat_count),
            lax.rem(lon + lon_step + plan.lon_count, plan.lon_count),
        )

    barrier = pltpu.get_barrier_semaphore()
    for lat_step, lon_step, _, _ in exchanges:
        pl.semaphore_signal(
            barrier, inc=1, device_id=device(lat_step, lon_step), device_id_type=pl.DeviceIdType.MESH
        )
    own_feat = feat_ref.at[pl.ds(first_own, plan.own)]
    loads = []
    for index, (source, target) in enumerate(
        (
            (mesh_in, own_feat), (edges_in, edges_ref), (mask_in, mask_ref), (grid_in, grid_ref),
            (wq_in, wq_ref), (cot_in, cot_ref), (wo_in, wo_ref), (wk_in, wk_ref), (wv_in, wv_ref),
        )
    ):
        load = pltpu.make_async_copy(source, target, load_sem.at[index])
        load.start()
        loads.append(load)
    mesh_load, edges_load, mask_load, grid_load, wq_load, cot_load, wo_load, wk_load, wv_load = loads

    mesh_load.wait()
    pack = pack_matrix(plan)
    pack_ref[...] = mm(pack, own_feat[...]).astype(jnp.bfloat16)
    edges_load.wait()
    mask_load.wait()
    fill_slots(
        plan, lat * plan.mesh_rows, lon * plan.mesh_cols, edges_ref, mask_ref, slot_ref
    )
    pl.semaphore_wait(barrier, len(exchanges))
    corner, lon_rim = plan.corner, plan.lon_rim
    sent = []
    for index, (lat_step, lon_step, first, count) in enumerate(exchanges):
        if lon_step == 0:
            start = first_own + (plan.own - count if lat_step < 0 else 0)
            source = feat_ref.at[pl.ds(start, count)]
        else:
            start = lon_rim if lon_step < 0 else 0
            if lat_step < 0:
                start += lon_rim - count
            source = pack_ref.at[pl.ds(start, count)]
        copy = pltpu.make_async_remote_copy(
            src_ref=source,
            dst_ref=feat_ref.at[pl.ds(first, count)],
            send_sem=send_sem.at[index],
            recv_sem=recv_sem.at[index],
            device_id=device(-lat_step, -lon_step),
            device_id_type=pl.DeviceIdType.MESH,
        )
        sent.append(copy)
    above, beside, below = sent[:3], sent[3:5], sent[5:]
    for copy in above + beside:
        copy.start()

    grid_load.wait()
    wq_load.wait()

    def query_columns(columns):
        queries = mm(grid_ref[...], wq_ref[:, columns]).astype(jnp.bfloat16)
        q_ref[:, columns] = (queries.astype(jnp.float32) * plan.scale).astype(jnp.bfloat16)

    column_tiles(plan.width, query_columns)
    cot_load.wait()
    wo_load.wait()

    def d_columns(columns):
        d_ref[:, columns] = mm(cot_ref[...], wo_ref[columns, :], NT).astype(jnp.bfloat16)

    column_tiles(plan.width, d_columns)
    wk_load.wait()
    wv_load.wait()
    for copy in below:
        copy.start()

    def project(low, high):
        ranges = plan.block_ranges(low, high)
        feat = jnp.concatenate([feat_ref[nodes, :] for nodes in plan.node_ranges(low, high)], axis=0)
        count = feat.shape[0]
        to_blocks = block_permutation(plan, high - low, True)
        dk_half_ref[0:count, :] = mm(to_blocks, feat).astype(jnp.bfloat16)

        def pair_columns(columns):
            feat = dk_half_ref[0:count, :]
            for weight_ref, target_ref in ((wk_ref, k_ref), (wv_ref, v_ref)):
                rows = mm(feat, weight_ref[:, columns]).astype(jnp.bfloat16)
                first = 0
                for nodes in ranges:
                    size = nodes.stop - nodes.start
                    target_ref[nodes, columns] = rows[first : first + size]
                    first += size

        column_tiles(plan.width, pair_columns)

    def project_gradients(low, high):
        ranges = plan.node_ranges(low, high)
        from_blocks = block_permutation(plan, high - low, False)
        count = from_blocks.shape[0]
        for source_ref, half_ref in ((dk_ref, dk_half_ref), (dv_ref, dv_half_ref)):
            terms = jnp.concatenate(
                [source_ref[nodes, :] for nodes in plan.block_ranges(low, high)], axis=0
            )
            half_ref[0:count, :] = mm(from_blocks, terms.astype(jnp.bfloat16)).astype(jnp.bfloat16)

        def part_columns(columns):
            part = mm(dk_half_ref[0:count, :], wk_ref[columns, :], NT)
            part = part + mm(dv_half_ref[0:count, :], wv_ref[columns, :], NT)
            if low > 0:
                own_ref[:, columns] = part[: plan.own]
            part = part.astype(jnp.bfloat16)
            first = 0
            for nodes in ranges:
                size = nodes.stop - nodes.start
                part_ref[nodes, columns] = part[first : first + size]
                first += size

        column_tiles(plan.width, part_columns)

    returned = []
    for index, (lat_step, lon_step, first, count) in enumerate(exchanges):
        if lon_step == 0:
            start = count if lat_step < 0 else 0
        else:
            base = 2 * plan.lat_rim
            if lat_step == 0:
                start = base + (lon_rim if lon_step < 0 else 0)
            else:
                base += 2 * lon_rim
                order = (0 if lon_step > 0 else 2) + (1 if lat_step < 0 else 0)
                start = base + order * corner
        copy = pltpu.make_async_remote_copy(
            src_ref=part_ref.at[pl.ds(first, count)],
            dst_ref=back_ref.at[pl.ds(start, count)],
            send_sem=back_send_sem.at[index],
            recv_sem=back_recv_sem.at[index],
            device_id=device(lat_step, lon_step),
            device_id_type=pl.DeviceIdType.MESH,
        )
        returned.append(copy)

    padded_rows = plan.mesh_rows + 2 * reach

    def at_middle():
        for copy in below:
            copy.wait()
        project(plan.mesh_rows + reach, padded_rows)
        project_gradients(0, reach)
        for copy in returned[:3]:
            copy.start()

    for copy in above + beside:
        copy.wait()
    project(0, plan.mesh_rows + reach)
    attend_tiles(
        plan, slot_ref, q_ref, d_ref, k_ref, v_ref, att_ref, dq_ref, dk_ref, dv_ref, bias_ref,
        at_middle,
    )
    project_gradients(reach, padded_rows)
    for copy in returned[3:]:
        copy.start()

    def out_columns(columns):
        out = grid_ref[:, columns].astype(jnp.float32) + mm(att_ref[...], wo_ref[:, columns])
        out_ref[:, columns] = out.astype(jnp.bfloat16)
        grad = cot_ref[:, columns].astype(jnp.float32) + mm(dq_ref[...], wq_ref[columns, :], NT)
        grid_grad_ref[:, columns] = grad.astype(jnp.bfloat16)

    column_tiles(plan.width, out_columns)
    stores = [
        pltpu.make_async_copy(out_ref, out_hbm, store_sem.at[0]),
        pltpu.make_async_copy(grid_grad_ref, grid_grad_hbm, store_sem.at[1]),
        pltpu.make_async_copy(mesh_grad_ref, mesh_grad_hbm, store_sem.at[2]),
    ]
    stores[0].start()
    stores[1].start()
    for copy in returned:
        copy.wait()
    corners = [
        pack[0:corner], pack[lon_rim - corner : lon_rim],
        pack[lon_rim : lon_rim + corner], pack[2 * lon_rim - corner : 2 * lon_rim],
    ]
    unpack = jnp.concatenate([pack] + corners, axis=0)
    lat_terms = 2 * plan.lat_rim
    last_rim = pl.ds(plan.own - plan.lat_rim, plan.lat_rim)

    def mesh_columns(columns):
        total = own_ref[:, columns] + mm(unpack, back_ref[lat_terms:, columns], TN)
        own_ref[:, columns] = total
        for start, rows in ((0, pl.ds(0, plan.lat_rim)), (plan.lat_rim, last_rim)):
            own_ref[rows, columns] += back_ref[pl.ds(start, plan.lat_rim), columns].astype(
                jnp.float32
            )
        mesh_grad_ref[:, columns] = own_ref[:, columns].astype(jnp.bfloat16)

    column_tiles(plan.width, mesh_columns)
    stores[2].start()
    for store in stores:
        store.wait()


def store_kernel(rows, *refs):
    sources, targets, held = refs[:3], refs[3:6], refs[6:9]
    load_sem, store_sem = refs[9:]
    loads, stores = [], []
    for source, target, buffer in zip(sources, targets, held):
        for start in range(0, source.shape[0], rows):
            part = pl.ds(start, rows)
            index = len(loads)
            loads.append(
                pltpu.make_async_copy(source.at[part], buffer.at[part], load_sem.at[index])
            )
            stores.append(
                pltpu.make_async_copy(buffer.at[part], target.at[part], store_sem.at[index])
            )
    for load in loads:
        load.start()
    for load, store in zip(loads, stores):
        load.wait()
        store.start()
    for store in stores:
        store.wait()


def local(grid_feat, mesh_feat, edges, edge_mask, w_query, w_key, w_value, w_out, cotangent):
    grid_rows, grid_cols, width = grid_feat.shape
    mesh_rows, mesh_cols, _ = mesh_feat.shape
    plan = Plan(
        mesh_rows, mesh_cols, grid_rows, grid_cols, width, lax.axis_size("lat"), lax.axis_size("lon")
    )
    half, full = jnp.bfloat16, jnp.float32
    points, own, nodes = plan.points, plan.own, plan.nodes
    anywhere = pl.BlockSpec(memory_space=pl.ANY)
    hbm = pl.BlockSpec(memory_space=pltpu.HBM)
    back_rows = 2 * plan.lat_rim + 2 * plan.lon_rim + 4 * plan.corner
    square = (width, width)
    layer_out, grid_grad, mesh_grad = pl.pallas_call(
        functools.partial(layer_kernel, plan),
        out_shape=(
            jax.ShapeDtypeStruct((points, width), half),
            jax.ShapeDtypeStruct((points, width), half),
            jax.ShapeDtypeStruct((own, width), half),
        ),
        in_specs=[hbm] * 9,
        out_specs=(hbm,) * 3,
        scratch_shapes=[
            pltpu.VMEM((points, width), half),
            pltpu.VMEM((points, width), half),
            pltpu.VMEM((own, width), half),
            pltpu.VMEM((points, width), half),
            pltpu.VMEM((points, width), half),
            pltpu.VMEM(edges.shape, jnp.int32),
            pltpu.VMEM(edges.shape, jnp.int32),
            pltpu.VMEM(square, half),
            pltpu.VMEM(square, half),
            pltpu.VMEM(square, half),
            pltpu.VMEM(square, half),
            pltpu.VMEM((nodes, width), half),
            pltpu.VMEM((2 * plan.lon_rim, width), half),
            pltpu.VMEM((plan.tiles, EDGE_SLOTS, plan.tile_points), jnp.int32),
            pltpu.VMEM((points, width), half),
            pltpu.VMEM((points, width), half),
            pltpu.VMEM((nodes, width), half),
            pltpu.VMEM((nodes, width), half),
            pltpu.VMEM((points, width), half),
            pltpu.VMEM((points, width), half),
            pltpu.VMEM((nodes, width), full),
            pltpu.VMEM((nodes, width), full),
            pltpu.VMEM((nodes, width), half),
            pltpu.VMEM((nodes, width), half),
            pltpu.VMEM((plan.keys, plan.tile_points), full),
            pltpu.VMEM((own, width), full),
            pltpu.VMEM((nodes, width), half),
            pltpu.VMEM((back_rows, width), half),
            pltpu.SemaphoreType.DMA((9,)),
            pltpu.SemaphoreType.DMA((3,)),
            pltpu.SemaphoreType.DMA((8,)),
            pltpu.SemaphoreType.DMA((8,)),
            pltpu.SemaphoreType.DMA((8,)),
            pltpu.SemaphoreType.DMA((8,)),
        ],
        compiler_params=pltpu.CompilerParams(
            collective_id=0, has_side_effects=True, vmem_limit_bytes=64 * 2**20
        ),
        cost_estimate=pl.CostEstimate(
            flops=8 * points * width * width + 8 * nodes * width * width,
            bytes_accessed=8 * width * width + 8 * points * width,
            transcendentals=points * plan.keys * HEAD_COUNT,
        ),
    )(
        grid_feat.reshape(points, width), mesh_feat.reshape(own, width), edges, edge_mask,
        w_query, w_key, w_value, w_out, cotangent.reshape(points, width),
    )
    results = (layer_out, grid_grad, mesh_grad)
    layer_out, grid_grad, mesh_grad = pl.pallas_call(
        functools.partial(store_kernel, own),
        out_shape=tuple(jax.ShapeDtypeStruct(x.shape, x.dtype) for x in results),
        in_specs=[anywhere] * 3,
        out_specs=(hbm,) * 3,
        scratch_shapes=[pltpu.VMEM(x.shape, x.dtype) for x in results]
        + [pltpu.SemaphoreType.DMA((2 * points // own + 1,))] * 2,
        compiler_params=pltpu.CompilerParams(vmem_limit_bytes=64 * 2**20),
    )(*results)
    return (
        layer_out.reshape(grid_feat.shape),
        grid_grad.reshape(grid_feat.shape),
        mesh_grad.reshape(mesh_feat.shape),
    )


def solution(mesh):
    placed = (
        P("lat", "lon", None),
        P("lat", "lon", None),
        P(None, "lat", "lon"),
        P(None, "lat", "lon"),
        P(),
        P(),
        P(),
        P(),
        P("lat", "lon", None),
    )
    return jax.shard_map(
        local,
        mesh=mesh,
        in_specs=placed,
        out_specs=(P("lat", "lon", None), P("lat", "lon", None), P("lat", "lon", None)),
        check_vma=False,
    )
```

```python
import functools
import math

import jax
import jax.numpy as jnp
from jax import lax
from jax.experimental import pallas as pl
from jax.experimental.pallas import tpu as pltpu
from jax.sharding import PartitionSpec as P

HEAD_COUNT = 16
EDGE_SLOTS = 12
HALO_REACH = 4
TILE_MESH_ROWS = 4
ROW_GROUP = 16
NEG_FILL = -1e30

NN = (((1,), (0,)), ((), ()))
NT = (((1,), (1,)), ((), ()))
TN = (((0,), (0,)), ((), ()))


def mm(a, b, dims=NN):
    return lax.dot_general(a, b, dims, preferred_element_type=jnp.float32)


class Plan:
    def __init__(self, mesh_rows, mesh_cols, grid_rows, grid_cols, width, lat_count, lon_count):
        reach = HALO_REACH
        self.mesh_rows, self.mesh_cols = mesh_rows, mesh_cols
        self.grid_rows, self.grid_cols, self.width = grid_rows, grid_cols, width
        self.lat_count, self.lon_count = lat_count, lon_count
        self.head = width // HEAD_COUNT
        self.scale = 1.0 / math.sqrt(self.head)
        self.points = grid_rows * grid_cols
        self.own = mesh_rows * mesh_cols
        padded_rows = mesh_rows + 2 * reach
        self.mid = padded_rows * mesh_cols
        self.strip = padded_rows * reach
        self.nodes = self.mid + 2 * self.strip
        self.lat_rim = reach * mesh_cols
        self.lon_rim = mesh_rows * reach
        self.corner = reach * reach
        self.block_cols = 2 * reach
        self.blocks = (mesh_cols + 2 * reach) // self.block_cols
        self.block = padded_rows * self.block_cols
        self.col_tiles = mesh_cols // self.block_cols
        self.row_tiles = mesh_rows // TILE_MESH_ROWS
        self.tiles = self.row_tiles * self.col_tiles
        self.tile_grid_rows = grid_rows // self.row_tiles
        self.tile_grid_cols = grid_cols // self.col_tiles
        self.tile_points = self.tile_grid_rows * self.tile_grid_cols
        self.row_step = TILE_MESH_ROWS * self.block_cols
        self.side_keys = (TILE_MESH_ROWS + 2 * reach) * self.block_cols
        self.keys = 2 * self.side_keys
        self.early = (mesh_rows - reach) // TILE_MESH_ROWS * self.col_tiles

    def node_ranges(self, low, high):
        reach, cols = HALO_REACH, self.mesh_cols
        right = self.mid + self.strip
        return (
            slice(low * cols, high * cols),
            slice(self.mid + low * reach, self.mid + high * reach),
            slice(right + low * reach, right + high * reach),
        )

    def block_ranges(self, low, high):
        return tuple(
            slice(
                block * self.block + low * self.block_cols,
                block * self.block + high * self.block_cols,
            )
            for block in range(self.blocks)
        )

    def exchanges(self):
        mid, strip = self.mid, self.strip
        corner, lon_rim, lat_rim = self.corner, self.lon_rim, self.lat_rim
        left, right = mid, mid + strip
        return (
            (-1, 0, 0, lat_rim),
            (-1, -1, left, corner),
            (-1, 1, right, corner),
            (0, -1, left + corner, lon_rim),
            (0, 1, right + corner, lon_rim),
            (1, 0, mid - lat_rim, lat_rim),
            (1, -1, left + strip - corner, corner),
            (1, 1, right + strip - corner, corner),
        )


def pack_matrix(plan):
    rows = 2 * plan.lon_rim
    row = lax.broadcasted_iota(jnp.int32, (rows, plan.own), 0)
    node = lax.broadcasted_iota(jnp.int32, (rows, plan.own), 1)
    is_right = (row >= plan.lon_rim).astype(jnp.int32)
    within = row - is_right * plan.lon_rim
    mesh_row = within // HALO_REACH
    col = within - mesh_row * HALO_REACH + is_right * (plan.mesh_cols - HALO_REACH)
    hit = node == mesh_row * plan.mesh_cols + col
    return hit.astype(jnp.float32).astype(jnp.bfloat16)


def block_permutation(plan, rows, to_blocks):
    reach, cols, wide = HALO_REACH, plan.mesh_cols, plan.block_cols
    count = rows * (cols + 2 * reach)
    vector = (count, 1) if to_blocks else (1, count)
    node = lax.broadcasted_iota(jnp.int32, vector, 0 if to_blocks else 1)
    block = jnp.zeros_like(node)
    for edge in range(1, plan.blocks):
        block = block + (node >= edge * rows * wide).astype(jnp.int32)
    within = node - block * (rows * wide)
    row = within // wide
    col = within - row * wide + block * wide
    left = rows * cols + row * reach + col
    middle = row * cols + col - reach
    right = left + rows * reach - reach - cols
    place = jnp.where(col < reach, left, jnp.where(col < reach + cols, middle, right))
    other = lax.broadcasted_iota(jnp.int32, (count, count), 1 if to_blocks else 0)
    return (other == place).astype(jnp.float32).astype(jnp.bfloat16)


def fill_slots(plan, lat_start, lon_start, edges_ref, mask_ref, slot_ref):
    reach, wide = HALO_REACH, plan.block_cols
    lon_total = plan.mesh_cols * plan.lon_count
    target = edges_ref[...]
    row_tile = lax.broadcasted_iota(jnp.int32, target.shape, 1) // plan.tile_grid_rows
    col_tile = lax.broadcasted_iota(jnp.int32, target.shape, 2) // plan.tile_grid_cols
    if lon_total & (lon_total - 1):
        node_row = lax.div(target, jnp.full_like(target, lon_total))
    else:
        node_row = lax.shift_right_logical(
            target, jnp.full_like(target, lon_total.bit_length() - 1)
        )
    node_col = target - node_row * lon_total - lon_start + reach
    node_col = jnp.where(node_col < 0, node_col + lon_total, node_col)
    node_col = jnp.where(node_col >= lon_total, node_col - lon_total, node_col)
    node_row = node_row - lat_start + reach - row_tile * TILE_MESH_ROWS
    node_col = node_col - col_tile * wide
    first = node_row * wide + node_col
    slots = jnp.where(node_col < wide, first, first + (plan.side_keys - wide))
    slots = jnp.where(mask_ref[...] > 0, slots, -1)
    for tile in range(plan.tiles):
        row, col = divmod(tile, plan.col_tiles)
        rows = range(row * plan.tile_grid_rows, (row + 1) * plan.tile_grid_rows)
        cols = slice(col * plan.tile_grid_cols, (col + 1) * plan.tile_grid_cols)
        slot_ref[tile] = jnp.concatenate([slots[:, row, cols] for row in rows], axis=1)


def attend_tiles(
    plan, slot_ref, q_ref, d_ref, k_ref, v_ref, att_ref, dq_ref, dk_ref, dv_ref, bias_ref,
    at_middle,
):
    head, tile_points = plan.head, plan.tile_points
    pair = 2 * head
    pairs = plan.width // pair
    low = (lax.broadcasted_iota(jnp.int32, (1, pair), 1) < head).astype(jnp.float32)
    high = (1.0 - low).astype(jnp.bfloat16)
    low = low.astype(jnp.bfloat16)
    dk_ref[...] = jnp.zeros_like(dk_ref)
    dv_ref[...] = jnp.zeros_like(dv_ref)

    def tile_step(tile, carry):
        pl.when(tile == plan.early)(at_middle)
        row_tile, col_tile = tile // plan.col_tiles, tile % plan.col_tiles
        first_point = (
            row_tile * (plan.tile_grid_rows * plan.grid_cols) + col_tile * plan.tile_grid_cols
        )
        segments = tuple(
            pl.ds(
                pl.multiple_of(first_point + row * plan.grid_cols, ROW_GROUP), plan.tile_grid_cols
            )
            for row in range(plan.tile_grid_rows)
        )
        first_key = col_tile * plan.block + row_tile * plan.row_step
        windows = tuple(
            (
                pl.ds(pl.multiple_of(first_key + side * plan.block, ROW_GROUP), plan.side_keys),
                side * plan.side_keys,
            )
            for side in range(2)
        )
        key_id = lax.broadcasted_iota(jnp.int32, (plan.keys, tile_points), 0)
        slots = slot_ref[tile]
        linked = key_id == slots[0:1]
        for slot in range(1, EDGE_SLOTS):
            linked = linked | (key_id == slots[slot : slot + 1])
        bias_ref[...] = jnp.where(linked, 0.0, NEG_FILL)

        def split(block):
            return jnp.concatenate([block * low, block * high], axis=0)

        def joined(both):
            kept = jnp.concatenate([both[:head, :tile_points], both[head:, tile_points:]], axis=0)
            return kept.astype(jnp.bfloat16).T

        def points_of(ref, lanes):
            return jnp.concatenate([ref[segment, lanes] for segment in segments], axis=0)

        def put_points(ref, lanes, block):
            wide = plan.tile_grid_cols
            for row, segment in enumerate(segments):
                ref[segment, lanes] = block[row * wide : (row + 1) * wide]

        def window_of(ref, lanes):
            return jnp.concatenate([ref[window, lanes] for window, _ in windows], axis=0)

        def add_window(ref, lanes, block):
            for window, first in windows:
                ref[window, lanes] += block[first : first + window.size]

        def first_products(index):
            lanes = slice(index * pair, (index + 1) * pair)
            q2 = split(points_of(q_ref, lanes))
            d2 = split(points_of(d_ref, lanes))
            k2 = window_of(k_ref, lanes)
            v2 = window_of(v_ref, lanes)
            return lanes, q2, d2, k2, v2, mm(k2, q2, NT), mm(v2, d2, NT)

        def rest(lanes, q2, d2, k2, v2, scores, d_prob):
            bias = bias_ref[...]
            scores = scores + jnp.concatenate([bias, bias], axis=1)
            exps = jnp.exp(scores - jnp.max(scores, axis=0, keepdims=True))
            prob = exps * (1.0 / jnp.sum(exps, axis=0, keepdims=True))
            half = prob.astype(jnp.bfloat16)
            centred = jnp.sum(prob * d_prob, axis=0, keepdims=True)
            d_score = (prob * (d_prob - centred)).astype(jnp.bfloat16)
            put_points(att_ref, lanes, joined(mm(v2, half, TN)))
            put_points(dq_ref, lanes, joined(mm(k2, d_score, TN) * plan.scale))
            add_window(dk_ref, lanes, mm(d_score, q2))
            add_window(dv_ref, lanes, mm(half, d2))

        ready = first_products(0)
        for index in range(pairs):
            following = first_products(index + 1) if index + 1 < pairs else None
            rest(*ready)
            ready = following
        return carry

    lax.fori_loop(0, plan.tiles, tile_step, 0)


def column_tiles(width, body):
    tile = min(width, 512)

    def step(index, carry):
        body(pl.ds(pl.multiple_of(index * tile, tile), tile))
        return carry

    lax.fori_loop(0, width // tile, step, 0)


def layer_kernel(
    plan,
    grid_in, mesh_in, edges_in, mask_in, wq_in, wk_in, wv_in, wo_in, cot_in,
    out_hbm, grid_grad_hbm, mesh_grad_hbm,
    out_ref, grid_grad_ref, mesh_grad_ref, grid_ref, cot_ref, edges_ref, mask_ref, wq_ref, wk_ref, wv_ref, wo_ref,
    feat_ref, pack_ref, slot_ref, q_ref, d_ref, k_ref, v_ref, att_ref, dq_ref,
    dk_ref, dv_ref, dk_half_ref, dv_half_ref, bias_ref, own_ref, part_ref, back_ref,
    load_sem, store_sem, send_sem, recv_sem, back_send_sem, back_recv_sem,
):
    reach = HALO_REACH
    lat, lon = lax.axis_index("lat"), lax.axis_index("lon")
    exchanges = plan.exchanges()
    first_own = plan.lat_rim

    def device(lat_step, lon_step):
        return (
            lax.rem(lat + lat_step + plan.lat_count, plan.lat_count),
            lax.rem(lon + lon_step + plan.lon_count, plan.lon_count),
        )

    barrier = pltpu.get_barrier_semaphore()
    for lat_step, lon_step, _, _ in exchanges:
        pl.semaphore_signal(
            barrier, inc=1, device_id=device(lat_step, lon_step), device_id_type=pl.DeviceIdType.MESH
        )
    own_feat = feat_ref.at[pl.ds(first_own, plan.own)]
    loads = []
    for index, (source, target) in enumerate(
        (
            (mesh_in, own_feat), (edges_in, edges_ref), (mask_in, mask_ref), (grid_in, grid_ref),
            (wq_in, wq_ref), (cot_in, cot_ref), (wo_in, wo_ref), (wk_in, wk_ref), (wv_in, wv_ref),
        )
    ):
        load = pltpu.make_async_copy(source, target, load_sem.at[index])
        load.start()
        loads.append(load)
    mesh_load, edges_load, mask_load, grid_load, wq_load, cot_load, wo_load, wk_load, wv_load = loads

    mesh_load.wait()
    pack = pack_matrix(plan)
    pack_ref[...] = mm(pack, own_feat[...]).astype(jnp.bfloat16)
    pl.semaphore_wait(barrier, len(exchanges))
    corner, lon_rim = plan.corner, plan.lon_rim
    sent = []
    for index, (lat_step, lon_step, first, count) in enumerate(exchanges):
        if lon_step == 0:
            start = first_own + (plan.own - count if lat_step < 0 else 0)
            source = feat_ref.at[pl.ds(start, count)]
        else:
            start = lon_rim if lon_step < 0 else 0
            if lat_step < 0:
                start += lon_rim - count
            source = pack_ref.at[pl.ds(start, count)]
        copy = pltpu.make_async_remote_copy(
            src_ref=source,
            dst_ref=feat_ref.at[pl.ds(first, count)],
            send_sem=send_sem.at[index],
            recv_sem=recv_sem.at[index],
            device_id=device(-lat_step, -lon_step),
            device_id_type=pl.DeviceIdType.MESH,
        )
        sent.append(copy)
    above, beside, below = sent[:3], sent[3:5], sent[5:]
    for copy in above + beside:
        copy.start()

    edges_load.wait()
    mask_load.wait()
    fill_slots(
        plan, lat * plan.mesh_rows, lon * plan.mesh_cols, edges_ref, mask_ref, slot_ref
    )
    grid_load.wait()
    wq_load.wait()

    def query_columns(columns):
        queries = mm(grid_ref[...], wq_ref[:, columns]).astype(jnp.bfloat16)
        q_ref[:, columns] = (queries.astype(jnp.float32) * plan.scale).astype(jnp.bfloat16)

    column_tiles(plan.width, query_columns)
    cot_load.wait()
    wo_load.wait()

    def d_columns(columns):
        d_ref[:, columns] = mm(cot_ref[...], wo_ref[columns, :], NT).astype(jnp.bfloat16)

    column_tiles(plan.width, d_columns)
    wk_load.wait()
    wv_load.wait()
    for copy in below:
        copy.start()

    def project(low, high):
        ranges = plan.block_ranges(low, high)
        feat = jnp.concatenate([feat_ref[nodes, :] for nodes in plan.node_ranges(low, high)], axis=0)
        count = feat.shape[0]
        to_blocks = block_permutation(plan, high - low, True)
        dk_half_ref[0:count, :] = mm(to_blocks, feat).astype(jnp.bfloat16)

        def pair_columns(columns):
            feat = dk_half_ref[0:count, :]
            for weight_ref, target_ref in ((wk_ref, k_ref), (wv_ref, v_ref)):
                rows = mm(feat, weight_ref[:, columns]).astype(jnp.bfloat16)
                first = 0
                for nodes in ranges:
                    size = nodes.stop - nodes.start
                    target_ref[nodes, columns] = rows[first : first + size]
                    first += size

        column_tiles(plan.width, pair_columns)

    def project_gradients(low, high):
        ranges = plan.node_ranges(low, high)
        from_blocks = block_permutation(plan, high - low, False)
        count = from_blocks.shape[0]
        for source_ref, half_ref in ((dk_ref, dk_half_ref), (dv_ref, dv_half_ref)):
            terms = jnp.concatenate(
                [source_ref[nodes, :] for nodes in plan.block_ranges(low, high)], axis=0
            )
            half_ref[0:count, :] = mm(from_blocks, terms.astype(jnp.bfloat16)).astype(jnp.bfloat16)

        def part_columns(columns):
            part = mm(dk_half_ref[0:count, :], wk_ref[columns, :], NT)
            part = part + mm(dv_half_ref[0:count, :], wv_ref[columns, :], NT)
            if low > 0:
                own_ref[:, columns] = part[: plan.own]
            part = part.astype(jnp.bfloat16)
            first = 0
            for nodes in ranges:
                size = nodes.stop - nodes.start
                part_ref[nodes, columns] = part[first : first + size]
                first += size

        column_tiles(plan.width, part_columns)

    returned = []
    for index, (lat_step, lon_step, first, count) in enumerate(exchanges):
        if lon_step == 0:
            start = count if lat_step < 0 else 0
        else:
            base = 2 * plan.lat_rim
            if lat_step == 0:
                start = base + (lon_rim if lon_step < 0 else 0)
            else:
                base += 2 * lon_rim
                order = (0 if lon_step > 0 else 2) + (1 if lat_step < 0 else 0)
                start = base + order * corner
        copy = pltpu.make_async_remote_copy(
            src_ref=part_ref.at[pl.ds(first, count)],
            dst_ref=back_ref.at[pl.ds(start, count)],
            send_sem=back_send_sem.at[index],
            recv_sem=back_recv_sem.at[index],
            device_id=device(lat_step, lon_step),
            device_id_type=pl.DeviceIdType.MESH,
        )
        returned.append(copy)

    padded_rows = plan.mesh_rows + 2 * reach

    def at_middle():
        for copy in below:
            copy.wait()
        project(plan.mesh_rows + reach, padded_rows)
        project_gradients(0, reach)
        for copy in returned[:3]:
            copy.start()

    for copy in above + beside:
        copy.wait()
    project(0, plan.mesh_rows + reach)
    attend_tiles(
        plan, slot_ref, q_ref, d_ref, k_ref, v_ref, att_ref, dq_ref, dk_ref, dv_ref, bias_ref,
        at_middle,
    )
    project_gradients(reach, padded_rows)
    for copy in returned[3:]:
        copy.start()

    def out_columns(columns):
        out = grid_ref[:, columns].astype(jnp.float32) + mm(att_ref[...], wo_ref[:, columns])
        out_ref[:, columns] = out.astype(jnp.bfloat16)
        grad = cot_ref[:, columns].astype(jnp.float32) + mm(dq_ref[...], wq_ref[columns, :], NT)
        grid_grad_ref[:, columns] = grad.astype(jnp.bfloat16)

    column_tiles(plan.width, out_columns)
    stores = [
        pltpu.make_async_copy(out_ref, out_hbm, store_sem.at[0]),
        pltpu.make_async_copy(grid_grad_ref, grid_grad_hbm, store_sem.at[1]),
        pltpu.make_async_copy(mesh_grad_ref, mesh_grad_hbm, store_sem.at[2]),
    ]
    stores[0].start()
    stores[1].start()
    for copy in returned:
        copy.wait()
    corners = [
        pack[0:corner], pack[lon_rim - corner : lon_rim],
        pack[lon_rim : lon_rim + corner], pack[2 * lon_rim - corner : 2 * lon_rim],
    ]
    unpack = jnp.concatenate([pack] + corners, axis=0)
    lat_terms = 2 * plan.lat_rim
    last_rim = pl.ds(plan.own - plan.lat_rim, plan.lat_rim)

    def mesh_columns(columns):
        total = own_ref[:, columns] + mm(unpack, back_ref[lat_terms:, columns], TN)
        own_ref[:, columns] = total
        for start, rows in ((0, pl.ds(0, plan.lat_rim)), (plan.lat_rim, last_rim)):
            own_ref[rows, columns] += back_ref[pl.ds(start, plan.lat_rim), columns].astype(
                jnp.float32
            )
        mesh_grad_ref[:, columns] = own_ref[:, columns].astype(jnp.bfloat16)

    column_tiles(plan.width, mesh_columns)
    stores[2].start()
    for store in stores:
        store.wait()


def store_kernel(rows, *refs):
    sources, targets, held = refs[:3], refs[3:6], refs[6:9]
    load_sem, store_sem = refs[9:]
    loads, stores = [], []
    for source, target, buffer in zip(sources, targets, held):
        for start in range(0, source.shape[0], rows):
            part = pl.ds(start, rows)
            index = len(loads)
            loads.append(
                pltpu.make_async_copy(source.at[part], buffer.at[part], load_sem.at[index])
            )
            stores.append(
                pltpu.make_async_copy(buffer.at[part], target.at[part], store_sem.at[index])
            )
    for load in loads:
        load.start()
    for load, store in zip(loads, stores):
        load.wait()
        store.start()
    for store in stores:
        store.wait()


def local(grid_feat, mesh_feat, edges, edge_mask, w_query, w_key, w_value, w_out, cotangent):
    grid_rows, grid_cols, width = grid_feat.shape
    mesh_rows, mesh_cols, _ = mesh_feat.shape
    plan = Plan(
        mesh_rows, mesh_cols, grid_rows, grid_cols, width, lax.axis_size("lat"), lax.axis_size("lon")
    )
    half, full = jnp.bfloat16, jnp.float32
    points, own, nodes = plan.points, plan.own, plan.nodes
    anywhere = pl.BlockSpec(memory_space=pl.ANY)
    hbm = pl.BlockSpec(memory_space=pltpu.HBM)
    back_rows = 2 * plan.lat_rim + 2 * plan.lon_rim + 4 * plan.corner
    square = (width, width)
    layer_out, grid_grad, mesh_grad = pl.pallas_call(
        functools.partial(layer_kernel, plan),
        out_shape=(
            jax.ShapeDtypeStruct((points, width), half),
            jax.ShapeDtypeStruct((points, width), half),
            jax.ShapeDtypeStruct((own, width), half),
        ),
        in_specs=[hbm] * 9,
        out_specs=(hbm,) * 3,
        scratch_shapes=[
            pltpu.VMEM((points, width), half),
            pltpu.VMEM((points, width), half),
            pltpu.VMEM((own, width), half),
            pltpu.VMEM((points, width), half),
            pltpu.VMEM((points, width), half),
            pltpu.VMEM(edges.shape, jnp.int32),
            pltpu.VMEM(edges.shape, jnp.int32),
            pltpu.VMEM(square, half),
            pltpu.VMEM(square, half),
            pltpu.VMEM(square, half),
            pltpu.VMEM(square, half),
            pltpu.VMEM((nodes, width), half),
            pltpu.VMEM((2 * plan.lon_rim, width), half),
            pltpu.VMEM((plan.tiles, EDGE_SLOTS, plan.tile_points), jnp.int32),
            pltpu.VMEM((points, width), half),
            pltpu.VMEM((points, width), half),
            pltpu.VMEM((nodes, width), half),
            pltpu.VMEM((nodes, width), half),
            pltpu.VMEM((points, width), half),
            pltpu.VMEM((points, width), half),
            pltpu.VMEM((nodes, width), full),
            pltpu.VMEM((nodes, width), full),
            pltpu.VMEM((nodes, width), half),
            pltpu.VMEM((nodes, width), half),
            pltpu.VMEM((plan.keys, plan.tile_points), full),
            pltpu.VMEM((own, width), full),
            pltpu.VMEM((nodes, width), half),
            pltpu.VMEM((back_rows, width), half),
            pltpu.SemaphoreType.DMA((9,)),
            pltpu.SemaphoreType.DMA((3,)),
            pltpu.SemaphoreType.DMA((8,)),
            pltpu.SemaphoreType.DMA((8,)),
            pltpu.SemaphoreType.DMA((8,)),
            pltpu.SemaphoreType.DMA((8,)),
        ],
        compiler_params=pltpu.CompilerParams(
            collective_id=0, has_side_effects=True, vmem_limit_bytes=64 * 2**20
        ),
        cost_estimate=pl.CostEstimate(
            flops=8 * points * width * width + 8 * nodes * width * width,
            bytes_accessed=8 * width * width + 8 * points * width,
            transcendentals=points * plan.keys * HEAD_COUNT,
        ),
    )(
        grid_feat.reshape(points, width), mesh_feat.reshape(own, width), edges, edge_mask,
        w_query, w_key, w_value, w_out, cotangent.reshape(points, width),
    )
    results = (layer_out, grid_grad, mesh_grad)
    layer_out, grid_grad, mesh_grad = pl.pallas_call(
        functools.partial(store_kernel, own),
        out_shape=tuple(jax.ShapeDtypeStruct(x.shape, x.dtype) for x in results),
        in_specs=[anywhere] * 3,
        out_specs=(hbm,) * 3,
        scratch_shapes=[pltpu.VMEM(x.shape, x.dtype) for x in results]
        + [pltpu.SemaphoreType.DMA((2 * points // own + 1,))] * 2,
        compiler_params=pltpu.CompilerParams(vmem_limit_bytes=64 * 2**20),
    )(*results)
    return (
        layer_out.reshape(grid_feat.shape),
        grid_grad.reshape(grid_feat.shape),
        mesh_grad.reshape(mesh_feat.shape),
    )


def solution(mesh):
    placed = (
        P("lat", "lon", None),
        P("lat", "lon", None),
        P(None, "lat", "lon"),
        P(None, "lat", "lon"),
        P(),
        P(),
        P(),
        P(),
        P("lat", "lon", None),
    )
    return jax.shard_map(
        local,
        mesh=mesh,
        in_specs=placed,
        out_specs=(P("lat", "lon", None), P("lat", "lon", None), P("lat", "lon", None)),
        check_vma=False,
    )
```

```python
import functools
import math

import jax
import jax.numpy as jnp
from jax import lax
from jax.experimental import pallas as pl
from jax.experimental.pallas import tpu as pltpu
from jax.sharding import PartitionSpec as P

HEAD_COUNT = 16
EDGE_SLOTS = 12
HALO_REACH = 4
TILE_MESH_ROWS = 4
ROW_GROUP = 16
NEG_FILL = -1e30

NN = (((1,), (0,)), ((), ()))
NT = (((1,), (1,)), ((), ()))
TN = (((0,), (0,)), ((), ()))


def mm(a, b, dims=NN):
    return lax.dot_general(a, b, dims, preferred_element_type=jnp.float32)


class Plan:
    def __init__(self, mesh_rows, mesh_cols, grid_rows, grid_cols, width, lat_count, lon_count):
        reach = HALO_REACH
        self.mesh_rows, self.mesh_cols = mesh_rows, mesh_cols
        self.grid_rows, self.grid_cols, self.width = grid_rows, grid_cols, width
        self.lat_count, self.lon_count = lat_count, lon_count
        self.head = width // HEAD_COUNT
        self.scale = 1.0 / math.sqrt(self.head)
        self.points = grid_rows * grid_cols
        self.own = mesh_rows * mesh_cols
        padded_rows = mesh_rows + 2 * reach
        self.mid = padded_rows * mesh_cols
        self.strip = padded_rows * reach
        self.nodes = self.mid + 2 * self.strip
        self.lat_rim = reach * mesh_cols
        self.lon_rim = mesh_rows * reach
        self.corner = reach * reach
        self.block_cols = 2 * reach
        self.blocks = (mesh_cols + 2 * reach) // self.block_cols
        self.block = padded_rows * self.block_cols
        self.col_tiles = mesh_cols // self.block_cols
        self.row_tiles = mesh_rows // TILE_MESH_ROWS
        self.tiles = self.row_tiles * self.col_tiles
        self.tile_grid_rows = grid_rows // self.row_tiles
        self.tile_grid_cols = grid_cols // self.col_tiles
        self.tile_points = self.tile_grid_rows * self.tile_grid_cols
        self.row_step = TILE_MESH_ROWS * self.block_cols
        self.side_keys = (TILE_MESH_ROWS + 2 * reach) * self.block_cols
        self.keys = 2 * self.side_keys
        self.early = (mesh_rows - reach) // TILE_MESH_ROWS * self.col_tiles

    def node_ranges(self, low, high):
        reach, cols = HALO_REACH, self.mesh_cols
        right = self.mid + self.strip
        return (
            slice(low * cols, high * cols),
            slice(self.mid + low * reach, self.mid + high * reach),
            slice(right + low * reach, right + high * reach),
        )

    def block_ranges(self, low, high):
        return tuple(
            slice(
                block * self.block + low * self.block_cols,
                block * self.block + high * self.block_cols,
            )
            for block in range(self.blocks)
        )

    def exchanges(self):
        mid, strip = self.mid, self.strip
        corner, lon_rim, lat_rim = self.corner, self.lon_rim, self.lat_rim
        left, right = mid, mid + strip
        return (
            (-1, 0, 0, lat_rim),
            (-1, -1, left, corner),
            (-1, 1, right, corner),
            (0, -1, left + corner, lon_rim),
            (0, 1, right + corner, lon_rim),
            (1, 0, mid - lat_rim, lat_rim),
            (1, -1, left + strip - corner, corner),
            (1, 1, right + strip - corner, corner),
        )


def pack_matrix(plan):
    rows = 2 * plan.lon_rim
    row = lax.broadcasted_iota(jnp.int32, (rows, plan.own), 0)
    node = lax.broadcasted_iota(jnp.int32, (rows, plan.own), 1)
    is_right = (row >= plan.lon_rim).astype(jnp.int32)
    within = row - is_right * plan.lon_rim
    mesh_row = within // HALO_REACH
    col = within - mesh_row * HALO_REACH + is_right * (plan.mesh_cols - HALO_REACH)
    hit = node == mesh_row * plan.mesh_cols + col
    return hit.astype(jnp.float32).astype(jnp.bfloat16)


def block_permutation(plan, rows, to_blocks):
    reach, cols, wide = HALO_REACH, plan.mesh_cols, plan.block_cols
    count = rows * (cols + 2 * reach)
    vector = (count, 1) if to_blocks else (1, count)
    node = lax.broadcasted_iota(jnp.int32, vector, 0 if to_blocks else 1)
    block = jnp.zeros_like(node)
    for edge in range(1, plan.blocks):
        block = block + (node >= edge * rows * wide).astype(jnp.int32)
    within = node - block * (rows * wide)
    row = within // wide
    col = within - row * wide + block * wide
    left = rows * cols + row * reach + col
    middle = row * cols + col - reach
    right = left + rows * reach - reach - cols
    place = jnp.where(col < reach, left, jnp.where(col < reach + cols, middle, right))
    other = lax.broadcasted_iota(jnp.int32, (count, count), 1 if to_blocks else 0)
    return (other == place).astype(jnp.float32).astype(jnp.bfloat16)


def fill_slots(plan, lat_start, lon_start, edges_ref, mask_ref, slot_ref):
    reach, wide = HALO_REACH, plan.block_cols
    lon_total = plan.mesh_cols * plan.lon_count
    target = edges_ref[...]
    row_tile = lax.broadcasted_iota(jnp.int32, target.shape, 1) // plan.tile_grid_rows
    col_tile = lax.broadcasted_iota(jnp.int32, target.shape, 2) // plan.tile_grid_cols
    if lon_total & (lon_total - 1):
        node_row = lax.div(target, jnp.full_like(target, lon_total))
    else:
        node_row = lax.shift_right_logical(
            target, jnp.full_like(target, lon_total.bit_length() - 1)
        )
    node_col = target - node_row * lon_total - lon_start + reach
    node_col = jnp.where(node_col < 0, node_col + lon_total, node_col)
    node_col = jnp.where(node_col >= lon_total, node_col - lon_total, node_col)
    node_row = node_row - lat_start + reach - row_tile * TILE_MESH_ROWS
    node_col = node_col - col_tile * wide
    first = node_row * wide + node_col
    slots = jnp.where(node_col < wide, first, first + (plan.side_keys - wide))
    slots = jnp.where(mask_ref[...] > 0, slots, -1)
    for tile in range(plan.tiles):
        row, col = divmod(tile, plan.col_tiles)
        rows = range(row * plan.tile_grid_rows, (row + 1) * plan.tile_grid_rows)
        cols = slice(col * plan.tile_grid_cols, (col + 1) * plan.tile_grid_cols)
        slot_ref[tile] = jnp.concatenate([slots[:, row, cols] for row in rows], axis=1)


def attend_tiles(
    plan, slot_ref, q_ref, d_ref, k_ref, v_ref, att_ref, dq_ref, dk_ref, dv_ref, bias_ref,
    at_middle,
):
    head, tile_points = plan.head, plan.tile_points
    pair = 2 * head
    pairs = plan.width // pair
    low = (lax.broadcasted_iota(jnp.int32, (1, pair), 1) < head).astype(jnp.float32)
    high = (1.0 - low).astype(jnp.bfloat16)
    low = low.astype(jnp.bfloat16)
    dk_ref[...] = jnp.zeros_like(dk_ref)
    dv_ref[...] = jnp.zeros_like(dv_ref)

    def tile_step(tile, carry):
        pl.when(tile == plan.early)(at_middle)
        row_tile, col_tile = tile // plan.col_tiles, tile % plan.col_tiles
        first_point = (
            row_tile * (plan.tile_grid_rows * plan.grid_cols) + col_tile * plan.tile_grid_cols
        )
        segments = tuple(
            pl.ds(
                pl.multiple_of(first_point + row * plan.grid_cols, ROW_GROUP), plan.tile_grid_cols
            )
            for row in range(plan.tile_grid_rows)
        )
        first_key = col_tile * plan.block + row_tile * plan.row_step
        windows = tuple(
            (
                pl.ds(pl.multiple_of(first_key + side * plan.block, ROW_GROUP), plan.side_keys),
                side * plan.side_keys,
            )
            for side in range(2)
        )
        key_id = lax.broadcasted_iota(jnp.int32, (plan.keys, tile_points), 0)
        slots = slot_ref[tile]
        linked = key_id == slots[0:1]
        for slot in range(1, EDGE_SLOTS):
            linked = linked | (key_id == slots[slot : slot + 1])
        bias_ref[...] = jnp.where(linked, 0.0, NEG_FILL)

        def split(block):
            return jnp.concatenate([block * low, block * high], axis=0)

        def joined(both):
            kept = jnp.concatenate([both[:head, :tile_points], both[head:, tile_points:]], axis=0)
            return kept.astype(jnp.bfloat16).T

        def points_of(ref, lanes):
            return jnp.concatenate([ref[segment, lanes] for segment in segments], axis=0)

        def put_points(ref, lanes, block):
            wide = plan.tile_grid_cols
            for row, segment in enumerate(segments):
                ref[segment, lanes] = block[row * wide : (row + 1) * wide]

        def window_of(ref, lanes):
            return jnp.concatenate([ref[window, lanes] for window, _ in windows], axis=0)

        def add_window(ref, lanes, block):
            for window, first in windows:
                ref[window, lanes] += block[first : first + window.size]

        def first_products(index):
            lanes = pl.ds(pl.multiple_of(index * pair, pair), pair)
            q2 = split(points_of(q_ref, lanes))
            d2 = split(points_of(d_ref, lanes))
            k2 = window_of(k_ref, lanes)
            v2 = window_of(v_ref, lanes)
            return lanes, q2, d2, k2, v2, mm(k2, q2, NT), mm(v2, d2, NT)

        def rest(lanes, q2, d2, k2, v2, scores, d_prob):
            bias = bias_ref[...]
            scores = scores + jnp.concatenate([bias, bias], axis=1)
            exps = jnp.exp(scores - jnp.max(scores, axis=0, keepdims=True))
            prob = exps * (1.0 / jnp.sum(exps, axis=0, keepdims=True))
            half = prob.astype(jnp.bfloat16)
            centred = jnp.sum(prob * d_prob, axis=0, keepdims=True)
            d_score = (prob * (d_prob - centred)).astype(jnp.bfloat16)
            put_points(att_ref, lanes, joined(mm(v2, half, TN)))
            put_points(dq_ref, lanes, joined(mm(k2, d_score, TN) * plan.scale))
            add_window(dk_ref, lanes, mm(d_score, q2))
            add_window(dv_ref, lanes, mm(half, d2))

        def two_pairs(index, inner):
            first = first_products(2 * index)
            second = first_products(2 * index + 1)
            rest(*first)
            rest(*second)
            return inner

        lax.fori_loop(0, pairs // 2, two_pairs, 0)
        return carry

    lax.fori_loop(0, plan.tiles, tile_step, 0)


def column_tiles(width, body):
    tile = min(width, 512)

    def step(index, carry):
        body(pl.ds(pl.multiple_of(index * tile, tile), tile))
        return carry

    lax.fori_loop(0, width // tile, step, 0)


def layer_kernel(
    plan,
    grid_in, mesh_in, edges_in, mask_in, wq_in, wk_in, wv_in, wo_in, cot_in,
    out_hbm, grid_grad_hbm, mesh_grad_hbm,
    out_ref, grid_grad_ref, mesh_grad_ref, grid_ref, cot_ref, edges_ref, mask_ref, wq_ref, wk_ref, wv_ref, wo_ref,
    feat_ref, pack_ref, slot_ref, q_ref, d_ref, k_ref, v_ref, att_ref, dq_ref,
    dk_ref, dv_ref, dk_half_ref, dv_half_ref, bias_ref, own_ref, part_ref, back_ref,
    load_sem, store_sem, send_sem, recv_sem, back_send_sem, back_recv_sem,
):
    reach = HALO_REACH
    lat, lon = lax.axis_index("lat"), lax.axis_index("lon")
    exchanges = plan.exchanges()
    first_own = plan.lat_rim

    def device(lat_step, lon_step):
        return (
            lax.rem(lat + lat_step + plan.lat_count, plan.lat_count),
            lax.rem(lon + lon_step + plan.lon_count, plan.lon_count),
        )

    barrier = pltpu.get_barrier_semaphore()
    for lat_step, lon_step, _, _ in exchanges:
        pl.semaphore_signal(
            barrier, inc=1, device_id=device(lat_step, lon_step), device_id_type=pl.DeviceIdType.MESH
        )
    own_feat = feat_ref.at[pl.ds(first_own, plan.own)]
    loads = []
    for index, (source, target) in enumerate(
        (
            (mesh_in, own_feat), (edges_in, edges_ref), (mask_in, mask_ref), (grid_in, grid_ref),
            (wq_in, wq_ref), (cot_in, cot_ref), (wo_in, wo_ref), (wk_in, wk_ref), (wv_in, wv_ref),
        )
    ):
        load = pltpu.make_async_copy(source, target, load_sem.at[index])
        load.start()
        loads.append(load)
    mesh_load, edges_load, mask_load, grid_load, wq_load, cot_load, wo_load, wk_load, wv_load = loads

    mesh_load.wait()
    pack = pack_matrix(plan)
    pack_ref[...] = mm(pack, own_feat[...]).astype(jnp.bfloat16)
    pl.semaphore_wait(barrier, len(exchanges))
    corner, lon_rim = plan.corner, plan.lon_rim
    sent = []
    for index, (lat_step, lon_step, first, count) in enumerate(exchanges):
        if lon_step == 0:
            start = first_own + (plan.own - count if lat_step < 0 else 0)
            source = feat_ref.at[pl.ds(start, count)]
        else:
            start = lon_rim if lon_step < 0 else 0
            if lat_step < 0:
                start += lon_rim - count
            source = pack_ref.at[pl.ds(start, count)]
        copy = pltpu.make_async_remote_copy(
            src_ref=source,
            dst_ref=feat_ref.at[pl.ds(first, count)],
            send_sem=send_sem.at[index],
            recv_sem=recv_sem.at[index],
            device_id=device(-lat_step, -lon_step),
            device_id_type=pl.DeviceIdType.MESH,
        )
        sent.append(copy)
    above, beside, below = sent[:3], sent[3:5], sent[5:]
    for copy in above + beside:
        copy.start()

    edges_load.wait()
    mask_load.wait()
    fill_slots(
        plan, lat * plan.mesh_rows, lon * plan.mesh_cols, edges_ref, mask_ref, slot_ref
    )
    grid_load.wait()
    wq_load.wait()

    def query_columns(columns):
        queries = mm(grid_ref[...], wq_ref[:, columns]).astype(jnp.bfloat16)
        q_ref[:, columns] = (queries.astype(jnp.float32) * plan.scale).astype(jnp.bfloat16)

    column_tiles(plan.width, query_columns)
    cot_load.wait()
    wo_load.wait()

    def d_columns(columns):
        d_ref[:, columns] = mm(cot_ref[...], wo_ref[columns, :], NT).astype(jnp.bfloat16)

    column_tiles(plan.width, d_columns)
    wk_load.wait()
    wv_load.wait()
    for copy in below:
        copy.start()

    def project(low, high):
        ranges = plan.block_ranges(low, high)
        feat = jnp.concatenate([feat_ref[nodes, :] for nodes in plan.node_ranges(low, high)], axis=0)
        count = feat.shape[0]
        to_blocks = block_permutation(plan, high - low, True)
        dk_half_ref[0:count, :] = mm(to_blocks, feat).astype(jnp.bfloat16)

        def pair_columns(columns):
            feat = dk_half_ref[0:count, :]
            for weight_ref, target_ref in ((wk_ref, k_ref), (wv_ref, v_ref)):
                rows = mm(feat, weight_ref[:, columns]).astype(jnp.bfloat16)
                first = 0
                for nodes in ranges:
                    size = nodes.stop - nodes.start
                    target_ref[nodes, columns] = rows[first : first + size]
                    first += size

        column_tiles(plan.width, pair_columns)

    def project_gradients(low, high):
        ranges = plan.node_ranges(low, high)
        from_blocks = block_permutation(plan, high - low, False)
        count = from_blocks.shape[0]
        for source_ref, half_ref in ((dk_ref, dk_half_ref), (dv_ref, dv_half_ref)):
            terms = jnp.concatenate(
                [source_ref[nodes, :] for nodes in plan.block_ranges(low, high)], axis=0
            )
            half_ref[0:count, :] = mm(from_blocks, terms.astype(jnp.bfloat16)).astype(jnp.bfloat16)

        def part_columns(columns):
            part = mm(dk_half_ref[0:count, :], wk_ref[columns, :], NT)
            part = part + mm(dv_half_ref[0:count, :], wv_ref[columns, :], NT)
            if low > 0:
                own_ref[:, columns] = part[: plan.own]
            part = part.astype(jnp.bfloat16)
            first = 0
            for nodes in ranges:
                size = nodes.stop - nodes.start
                part_ref[nodes, columns] = part[first : first + size]
                first += size

        column_tiles(plan.width, part_columns)

    returned = []
    for index, (lat_step, lon_step, first, count) in enumerate(exchanges):
        if lon_step == 0:
            start = count if lat_step < 0 else 0
        else:
            base = 2 * plan.lat_rim
            if lat_step == 0:
                start = base + (lon_rim if lon_step < 0 else 0)
            else:
                base += 2 * lon_rim
                order = (0 if lon_step > 0 else 2) + (1 if lat_step < 0 else 0)
                start = base + order * corner
        copy = pltpu.make_async_remote_copy(
            src_ref=part_ref.at[pl.ds(first, count)],
            dst_ref=back_ref.at[pl.ds(start, count)],
            send_sem=back_send_sem.at[index],
            recv_sem=back_recv_sem.at[index],
            device_id=device(lat_step, lon_step),
            device_id_type=pl.DeviceIdType.MESH,
        )
        returned.append(copy)

    padded_rows = plan.mesh_rows + 2 * reach

    def at_middle():
        for copy in below:
            copy.wait()
        project(plan.mesh_rows + reach, padded_rows)
        project_gradients(0, reach)
        for copy in returned[:3]:
            copy.start()

    for copy in above + beside:
        copy.wait()
    project(0, plan.mesh_rows + reach)
    attend_tiles(
        plan, slot_ref, q_ref, d_ref, k_ref, v_ref, att_ref, dq_ref, dk_ref, dv_ref, bias_ref,
        at_middle,
    )
    project_gradients(reach, padded_rows)
    for copy in returned[3:]:
        copy.start()

    def out_columns(columns):
        out = grid_ref[:, columns].astype(jnp.float32) + mm(att_ref[...], wo_ref[:, columns])
        out_ref[:, columns] = out.astype(jnp.bfloat16)
        grad = cot_ref[:, columns].astype(jnp.float32) + mm(dq_ref[...], wq_ref[columns, :], NT)
        grid_grad_ref[:, columns] = grad.astype(jnp.bfloat16)

    column_tiles(plan.width, out_columns)
    stores = [
        pltpu.make_async_copy(out_ref, out_hbm, store_sem.at[0]),
        pltpu.make_async_copy(grid_grad_ref, grid_grad_hbm, store_sem.at[1]),
        pltpu.make_async_copy(mesh_grad_ref, mesh_grad_hbm, store_sem.at[2]),
    ]
    stores[0].start()
    stores[1].start()
    for copy in returned:
        copy.wait()
    corners = [
        pack[0:corner], pack[lon_rim - corner : lon_rim],
        pack[lon_rim : lon_rim + corner], pack[2 * lon_rim - corner : 2 * lon_rim],
    ]
    unpack = jnp.concatenate([pack] + corners, axis=0)
    lat_terms = 2 * plan.lat_rim
    last_rim = pl.ds(plan.own - plan.lat_rim, plan.lat_rim)

    def mesh_columns(columns):
        total = own_ref[:, columns] + mm(unpack, back_ref[lat_terms:, columns], TN)
        own_ref[:, columns] = total
        for start, rows in ((0, pl.ds(0, plan.lat_rim)), (plan.lat_rim, last_rim)):
            own_ref[rows, columns] += back_ref[pl.ds(start, plan.lat_rim), columns].astype(
                jnp.float32
            )
        mesh_grad_ref[:, columns] = own_ref[:, columns].astype(jnp.bfloat16)

    column_tiles(plan.width, mesh_columns)
    stores[2].start()
    for store in stores:
        store.wait()


def store_kernel(rows, *refs):
    sources, targets, held = refs[:3], refs[3:6], refs[6:9]
    load_sem, store_sem = refs[9:]
    loads, stores = [], []
    for source, target, buffer in zip(sources, targets, held):
        for start in range(0, source.shape[0], rows):
            part = pl.ds(start, rows)
            index = len(loads)
            loads.append(
                pltpu.make_async_copy(source.at[part], buffer.at[part], load_sem.at[index])
            )
            stores.append(
                pltpu.make_async_copy(buffer.at[part], target.at[part], store_sem.at[index])
            )
    for load in loads:
        load.start()
    for load, store in zip(loads, stores):
        load.wait()
        store.start()
    for store in stores:
        store.wait()


def local(grid_feat, mesh_feat, edges, edge_mask, w_query, w_key, w_value, w_out, cotangent):
    grid_rows, grid_cols, width = grid_feat.shape
    mesh_rows, mesh_cols, _ = mesh_feat.shape
    plan = Plan(
        mesh_rows, mesh_cols, grid_rows, grid_cols, width, lax.axis_size("lat"), lax.axis_size("lon")
    )
    half, full = jnp.bfloat16, jnp.float32
    points, own, nodes = plan.points, plan.own, plan.nodes
    anywhere = pl.BlockSpec(memory_space=pl.ANY)
    hbm = pl.BlockSpec(memory_space=pltpu.HBM)
    back_rows = 2 * plan.lat_rim + 2 * plan.lon_rim + 4 * plan.corner
    square = (width, width)
    layer_out, grid_grad, mesh_grad = pl.pallas_call(
        functools.partial(layer_kernel, plan),
        out_shape=(
            jax.ShapeDtypeStruct((points, width), half),
            jax.ShapeDtypeStruct((points, width), half),
            jax.ShapeDtypeStruct((own, width), half),
        ),
        in_specs=[hbm] * 9,
        out_specs=(hbm,) * 3,
        scratch_shapes=[
            pltpu.VMEM((points, width), half),
            pltpu.VMEM((points, width), half),
            pltpu.VMEM((own, width), half),
            pltpu.VMEM((points, width), half),
            pltpu.VMEM((points, width), half),
            pltpu.VMEM(edges.shape, jnp.int32),
            pltpu.VMEM(edges.shape, jnp.int32),
            pltpu.VMEM(square, half),
            pltpu.VMEM(square, half),
            pltpu.VMEM(square, half),
            pltpu.VMEM(square, half),
            pltpu.VMEM((nodes, width), half),
            pltpu.VMEM((2 * plan.lon_rim, width), half),
            pltpu.VMEM((plan.tiles, EDGE_SLOTS, plan.tile_points), jnp.int32),
            pltpu.VMEM((points, width), half),
            pltpu.VMEM((points, width), half),
            pltpu.VMEM((nodes, width), half),
            pltpu.VMEM((nodes, width), half),
            pltpu.VMEM((points, width), half),
            pltpu.VMEM((points, width), half),
            pltpu.VMEM((nodes, width), full),
            pltpu.VMEM((nodes, width), full),
            pltpu.VMEM((nodes, width), half),
            pltpu.VMEM((nodes, width), half),
            pltpu.VMEM((plan.keys, plan.tile_points), full),
            pltpu.VMEM((own, width), full),
            pltpu.VMEM((nodes, width), half),
            pltpu.VMEM((back_rows, width), half),
            pltpu.SemaphoreType.DMA((9,)),
            pltpu.SemaphoreType.DMA((3,)),
            pltpu.SemaphoreType.DMA((8,)),
            pltpu.SemaphoreType.DMA((8,)),
            pltpu.SemaphoreType.DMA((8,)),
            pltpu.SemaphoreType.DMA((8,)),
        ],
        compiler_params=pltpu.CompilerParams(
            collective_id=0, has_side_effects=True, vmem_limit_bytes=64 * 2**20
        ),
        cost_estimate=pl.CostEstimate(
            flops=8 * points * width * width + 8 * nodes * width * width,
            bytes_accessed=8 * width * width + 8 * points * width,
            transcendentals=points * plan.keys * HEAD_COUNT,
        ),
    )(
        grid_feat.reshape(points, width), mesh_feat.reshape(own, width), edges, edge_mask,
        w_query, w_key, w_value, w_out, cotangent.reshape(points, width),
    )
    results = (layer_out, grid_grad, mesh_grad)
    layer_out, grid_grad, mesh_grad = pl.pallas_call(
        functools.partial(store_kernel, own),
        out_shape=tuple(jax.ShapeDtypeStruct(x.shape, x.dtype) for x in results),
        in_specs=[anywhere] * 3,
        out_specs=(hbm,) * 3,
        scratch_shapes=[pltpu.VMEM(x.shape, x.dtype) for x in results]
        + [pltpu.SemaphoreType.DMA((2 * points // own + 1,))] * 2,
        compiler_params=pltpu.CompilerParams(vmem_limit_bytes=64 * 2**20),
    )(*results)
    return (
        layer_out.reshape(grid_feat.shape),
        grid_grad.reshape(grid_feat.shape),
        mesh_grad.reshape(mesh_feat.shape),
    )


def solution(mesh):
    placed = (
        P("lat", "lon", None),
        P("lat", "lon", None),
        P(None, "lat", "lon"),
        P(None, "lat", "lon"),
        P(),
        P(),
        P(),
        P(),
        P("lat", "lon", None),
    )
    return jax.shard_map(
        local,
        mesh=mesh,
        in_specs=placed,
        out_specs=(P("lat", "lon", None), P("lat", "lon", None), P("lat", "lon", None)),
        check_vma=False,
    )
```
